128 devices in a mesh: dp: 8 (over y_lo, z), factor: 16 (over x, y_hi, core).
Axes of the slice: x: 4, y: 4 (y_hi: 2, y_lo: 2; y = y_hi * 2 + y_lo), z: 4, core: 2. Of those that a mesh axis runs over, the one named last changes fastest.
Arguments:
- inputs: bfloat16 [3072, 16384], P('dp'), may hold values from -6 to 6
- first_factor: bfloat16 [16384, 2048], P(None, 'factor'), may hold values from -0.046875 to 0.046875
- second_factor: bfloat16 [2048, 26624], P('factor'), may hold values from -0.125 to 0.125
- out_grad: bfloat16 [3072, 26624], P('dp', 'factor'), may hold values from -0.59765625 to 0.59765625
Outputs:
- input_grad: bfloat16 [3072, 16384], P('dp', 'factor')
- first_grad: bfloat16 [16384, 2048], P('dp', 'factor')
- second_grad: bfloat16 [2048, 26624], P('factor', 'dp')
The draws below stay inside these ranges and needn't reach their ends.
All inputs are finite; a program needn't handle non-finite values.
Results may differ from the reference program's by a relative error of at most 0.023.
Values may be sent and summed in bfloat16 or wider, within the bound.
A program may use at most 192 MiB of HBM per device.

```python
import jax
import jax.numpy as jnp
from jax import lax

D = 16384
F = 26624
R = 2048
TOK_DEV = 384
TOKENS = 3072
N_DP = 8


def raised(result, key, source, target, blocks, factor):
    def block_of(dim):
        return (jnp.arange(result.shape[dim]) // (result.shape[dim] // blocks)).reshape((-1,) + (1,) * (result.ndim - 1 - dim))

    first = jax.random.permutation(key, blocks)[block_of(target)]
    second = (block_of(target) + blocks // 2) % blocks
    return jnp.where((block_of(source) == first) | (block_of(source) == second), factor * result, result)


def levels(rng, extent, shards, smallest, largest):
    level, own = 1.0, jax.random.fold_in(rng, 6)
    for position, blocks in shards:
        steps = jnp.exp(jax.random.uniform(jax.random.fold_in(own, position), (blocks,), jnp.float32, smallest / len(shards), largest / len(shards)))
        level = level * jnp.repeat(steps, extent[position] // blocks).reshape([-1 if axis == position else 1 for axis in range(len(extent))])
    return level


def bell_draw(key, extent, deviation, limit, pieces=(), dtype=jnp.bfloat16):
    level = levels(key, extent, pieces, -0.22, 0.18) if pieces else 1.0
    entries = jax.random.normal(key, extent, jnp.float32) * deviation * level
    return jnp.minimum(jnp.maximum(entries, -limit), limit).astype(dtype)


def heavy_noise(stream_key, dims, spread, limit, shards, heavy, kind=jnp.bfloat16):
    result = spread * jax.random.normal(stream_key, dims, jnp.float32)
    if shards:
        result = result * levels(stream_key, dims, shards, -0.22, 0.18)
    return jnp.clip(raised(result, jax.random.fold_in(stream_key, 3), *heavy), -limit, limit).astype(kind)


def setup_inputs(seed: int = 0) -> dict:
    arg_keys = jax.random.split(jax.random.key(seed), 5)
    return {
        "inputs": heavy_noise(arg_keys[0], (TOKENS, D), 1.0, 6.0, ((0, 8),), (0, 1, 8, 2.0)),
        "first_factor": bell_draw(arg_keys[1], (D, R), D ** -0.5, 0.046875, ((1, 16),)),
        "second_factor": bell_draw(arg_keys[2], (R, F), R ** -0.5, 0.125, ((0, 16),)),
        "out_grad": heavy_noise(arg_keys[3], (TOKENS, F), 0.1, 0.59765625, ((0, 8), (1, 16)), (0, 1, 16, 2.0)),
    }


def group_sum(left, right):
    total = jnp.zeros((left.shape[1], right.shape[1]), jnp.float32)
    for group in range(N_DP):
        rows_left = left[group * TOK_DEV:(group + 1) * TOK_DEV]
        rows_right = right[group * TOK_DEV:(group + 1) * TOK_DEV]
        term = jnp.dot(rows_left.T, rows_right, preferred_element_type=jnp.float32).astype(jnp.bfloat16)
        term = lax.optimization_barrier(term)
        total = total + term.astype(jnp.float32)
    return total.astype(jnp.bfloat16)


def reference(inputs, first_factor, second_factor, out_grad):
    hidden = jnp.dot(inputs, first_factor, preferred_element_type=jnp.float32).astype(jnp.bfloat16)
    rank_grad = jnp.dot(out_grad, second_factor.T, preferred_element_type=jnp.float32).astype(jnp.bfloat16)
    input_grad = jnp.dot(rank_grad, first_factor.T, preferred_element_type=jnp.float32).astype(jnp.bfloat16)
    first_grad = group_sum(inputs, rank_grad)
    second_grad = group_sum(hidden, out_grad)
    return input_grad, first_grad, second_grad
```

```python
import functools

import jax
import jax.numpy as jnp
from jax import lax
from jax.experimental import pallas as pl
from jax.experimental.pallas import tpu as pltpu
from jax.sharding import PartitionSpec as P

MESH = pl.DeviceIdType.MESH
BF = jnp.bfloat16
F32 = jnp.float32
TOK = 384
D = 16384
RK = 128
CB = 1664
FB = 1024
DB = 2048


def ds(i, n):
    return pl.ds(pl.multiple_of(i * n, n), n)


def nn(a, b):
    return jnp.dot(a, b, preferred_element_type=F32)


def nt(a, b):
    return lax.dot_general(a, b, (((1,), (1,)), ((), ())), preferred_element_type=F32)


def kernel(
    inp, ff, sf, og,
    ig_out, fg_out, sg_out,
    i_v, ff_v, og_r, sf_r, ffx, ht, h_acc, rg_acc, rg_p, rg_r, rg_all,
    sg_p, sg_r, sg_s, fg_p, fg_r, ig_p, ig_r, rgt,
    i_sem, ff_sem,
    og_ss, og_rs, sf_ss, sf_rs, fx_ss, fx_rs, h_ss, h_rs, rg_ss, rg_rs, ra_ss, ra_rs,
    sg_ss, sg_rs, c8_ss, c8_rs, fg_ss, fg_rs, ig_ss, ig_rs,
):
    d = lax.axis_index("dp")
    f = lax.axis_index("factor")
    yl, z = d // 4, d % 4
    x, yh, c = f // 4, (f // 2) % 2, f % 2
    y = 2 * yh + yl
    r4 = yh * 2 + c
    line = y * 2 + c

    def dev(x_, y_, z_, c_):
        return ((y_ % 2) * 4 + z_, x_ * 4 + (y_ // 2) * 2 + c_)

    def remote(src, dst, ss, rs, to):
        return pltpu.make_async_remote_copy(
            src_ref=src, dst_ref=dst, send_sem=ss, recv_sem=rs, device_id=to, device_id_type=MESH
        )

    def arrived(dst, rs):
        pltpu.make_async_copy(dst, dst, rs).wait()

    c8_to = [(x, 2 * (z // 2) + s, 2 * c + yh, z % 2) for s in range(2)]
    c8_from = [(x, 2 * (z % 2) + s, 2 * yh + c, z // 2) for s in range(2)]

    def is_me(t):
        return (t[1] == y) & (t[2] == z) & (t[3] == c)

    barrier = pltpu.get_barrier_semaphore()

    def greet(*t):
        pl.semaphore_signal(barrier, inc=1, device_id=dev(*t), device_id_type=MESH)

    for j in range(1, 8):
        other = (line + j) % 8
        greet(x, other // 2, z, other % 2)
    for k in range(1, 4):
        for yy in range(2):
            for cc in range(2):
                greet((x + k) % 4, 2 * yh + yy, z, cc)
    for k in range(1, 4):
        for yy in range(2):
            greet(x, 2 * yh + yy, (z + k) % 4, c)
    extra = 0
    for t in c8_to + c8_from:
        away = jnp.logical_not(is_me(t))

        @pl.when(away)
        def _(t=t):
            greet(*t)

        extra = extra + away.astype(jnp.int32)
    pl.semaphore_wait(barrier, 25 + extra)

    og_self = (c == yl) & (x % 2 == c)
    og_dst = og_r.at[ds(yl, TOK), ds(x // 2, CB)]
    og_rsem = og_rs.at[(x // 2) * 2 + yl]
    og_copies = [
        remote(og, og_dst, og_ss.at[k], og_rsem, dev((x + k) % 4, 2 * yh + c, z, x % 2))
        for k in range(4)
    ]
    og_local = pltpu.make_async_copy(og, og_dst, og_rsem)
    for k in (2, 1, 3):
        og_copies[k].start()

    @pl.when(jnp.logical_not(og_self))
    def _():
        og_copies[0].start()

    @pl.when(og_self)
    def _():
        og_local.start()

    ff_loads = [pltpu.make_async_copy(ff.at[k], ff_v.at[k], ff_sem.at[k]) for k in range(4)]
    i_loads = [
        pltpu.make_async_copy(inp.at[:, k * 4096 : (k + 1) * 4096], i_v.at[:, k * 4096 : (k + 1) * 4096], i_sem.at[k])
        for k in range(4)
    ]
    for k in range(4):
        ff_loads[k].start()
        i_loads[k].start()

    sends = []
    peers = [(y, 1 - c), (3 - y, 0), (3 - y, 1)]

    def sf_src(y_, c_, s):
        return sf.at[:, ds((2 * s + c_) * 4 + (y_ // 2) * 2 + y_ % 2, CB)]

    def sf_dst(s):
        return sf_r.at[ds(r4, RK), s * CB : (s + 1) * CB]

    for s in range(2):
        pltpu.make_async_copy(sf_src(y, c, s), sf_dst(s), sf_rs.at[r4 * 2 + s]).start()
        for n, (y_, c_) in enumerate(peers):
            cp = remote(sf_src(y_, c_, s), sf_dst(s), sf_ss.at[n * 2 + s], sf_rs.at[r4 * 2 + s], dev(x, y_, z, c_))
            cp.start()
            sends.append(cp)

    for k in range(4):
        ff_loads[k].wait()
        i_loads[k].wait()

        def h_step(j, _, k=k):
            h_acc[...] += nn(i_v[:, ds(k * 4 + j, FB)], ff_v[k, j])
            return 0

        if k == 0:
            h_acc[...] = jnp.zeros_like(h_acc)
        lax.fori_loop(0, 4, h_step, 0)
    ht_mine = ht.at[ds(r4, RK), ds(yl, TOK)]
    ht_mine[...] = h_acc[...].T.astype(BF)
    for j in range(1, 8):
        other = (line + j) % 8
        cp = remote(ht_mine, ht_mine, h_ss.at[j], h_rs.at[line], dev(x, other // 2, z, other % 2))
        cp.start()
        sends.append(cp)

    def fx_dst():
        return ffx.at[:, :, ds(r4, RK)]

    pltpu.make_async_copy(ff.at[:, r4], fx_dst(), fx_rs.at[r4]).start()
    for n, (y_, c_) in enumerate(peers):
        cp = remote(ff.at[:, (y_ // 2) * 2 + c_], fx_dst(), fx_ss.at[n], fx_rs.at[r4], dev(x, y_, z, c_))
        cp.start()
        sends.append(cp)

    for s in range(2):
        for q in range(4):
            arrived(sf_r.at[q * RK : (q + 1) * RK, s * CB : (s + 1) * CB], sf_rs.at[q * 2 + s])

    def rg_block(s):
        for t in range(2):
            arrived(og_r.at[t * TOK : (t + 1) * TOK, s * CB : (s + 1) * CB], og_rs.at[s * 2 + t])

            def step(n, _, t=t):
                part = nt(og_r[t * TOK : (t + 1) * TOK, s * CB : (s + 1) * CB], sf_r[ds(n, 256), s * CB : (s + 1) * CB])
                if s == 0:
                    rg_acc[t, n] = part
                else:
                    rg_p[t, :, ds(n, 256)] = (rg_acc[t, n] + part).astype(BF)
                return 0

            lax.fori_loop(0, 2, step, 0)

    def sg_block(s):
        def step(k, _):
            q = (z + k) % 4
            sg_p[q, :, s * CB : (s + 1) * CB] = nn(ht[ds(q, RK), :], og_r[:, s * CB : (s + 1) * CB]).astype(BF)

            @pl.when(k != 0)
            def _():
                remote(
                    sg_p.at[q, :, s * CB : (s + 1) * CB], sg_r.at[z, :, s * CB : (s + 1) * CB],
                    sg_ss.at[k * 2 + s], sg_rs.at[z * 2 + s], dev(x, y, q, c),
                ).start()

            return 0

        lax.fori_loop(0, 4, step, 0)

    rg_block(0)
    for j in range(1, 8):
        other = (line + j) % 8
        y_, c_ = other // 2, other % 2
        arrived(ht.at[ds((y_ // 2) * 2 + c_, RK), ds(y_ % 2, TOK)], h_rs.at[other])
    sg_block(0)
    rg_block(1)
    for j in range(1, 8):
        other = (line + j) % 8
        y_, c_ = other // 2, other % 2
        cp = remote(
            rg_p.at[y_ % 2, :, ds((y_ // 2) * 2 + c_, RK)], rg_r.at[line], rg_ss.at[j], rg_rs.at[line],
            dev(x, y_, z, c_),
        )
        cp.start()
        sends.append(cp)
    sg_block(1)

    total = rg_p[yl, :, ds(r4, RK)].astype(F32)
    for j in range(1, 8):
        other = (line + j) % 8
        arrived(rg_r.at[other], rg_rs.at[other])
        total = total + rg_r[other].astype(F32)
    rg_mine = rg_all.at[:, ds(r4, RK)]
    rg_mine[...] = total.astype(BF)
    for n, (y_, c_) in enumerate([(y, 1 - c), ((y + 2) % 4, 0), ((y + 2) % 4, 1)]):
        cp = remote(rg_mine, rg_mine, ra_ss.at[n], ra_rs.at[r4], dev(x, y_, z, c_))
        cp.start()
        sends.append(cp)
    rgt[...] = total.T.astype(BF)

    def fg_step(k, _):
        to = (d + k) % 8
        fg_p[to] = nn(rgt[...], i_v[:, ds(to, DB)]).astype(BF)

        @pl.when(k != 8)
        def _():
            remote(fg_p.at[to], fg_r.at[d], fg_ss.at[k - 1], fg_rs.at[d], (to, f)).start()

        return 0

    lax.fori_loop(1, 9, fg_step, 0)

    for j in range(4):
        arrived(ffx.at[:, :, j * RK : (j + 1) * RK], fx_rs.at[j])
    for j in range(1, 4):
        other = (r4 + j) % 4
        arrived(rg_all.at[:, ds(other, RK)], ra_rs.at[other])

    def ig_step(k, _):
        to = (x + k) % 4
        ig_p[to] = nt(rg_all[...], ffx[to]).astype(BF)

        @pl.when(k != 4)
        def _():
            remote(ig_p.at[to], ig_r.at[x], ig_ss.at[k - 1], ig_rs.at[x], dev(to, y, z, c)).start()

        return 0

    lax.fori_loop(1, 5, ig_step, 0)

    c8_copies = []
    for s in range(2):
        cols = slice(s * CB, (s + 1) * CB)
        total = sg_p[z, :, cols].astype(F32)
        for j in range(1, 4):
            other = (z + j) % 4
            arrived(sg_r.at[other, :, cols], sg_rs.at[other * 2 + s])
            total = total + sg_r[other, :, cols].astype(F32)
        sg_s[:, cols] = total.astype(BF)
        dst = sg_out.at[:, ds(yl, CB)]
        far = remote(sg_s.at[:, cols], dst, c8_ss.at[s], c8_rs.at[yl], dev(*c8_to[s]))
        near = pltpu.make_async_copy(sg_s.at[:, cols], dst, c8_rs.at[yl])

        @pl.when(jnp.logical_not(is_me(c8_to[s])))
        def _(far=far):
            far.start()

        @pl.when(is_me(c8_to[s]))
        def _(near=near):
            near.start()

        c8_copies.append(far)

    for j in range(1, 4):
        other = (x + j) % 4
        arrived(ig_r.at[other], ig_rs.at[other])

    def ig_sum(k, _):
        rows = ds(k, 64)
        acc = ig_p[x, rows, :].astype(F32)
        for j in range(1, 4):
            acc = acc + ig_r[(x + j) % 4, rows, :].astype(F32)
        ig_out[rows, :] = acc.astype(BF)
        return 0

    lax.fori_loop(0, TOK // 64, ig_sum, 0)

    for j in range(1, 8):
        other = (d + j) % 8
        arrived(fg_r.at[other], fg_rs.at[other])

    def fg_sum(k, _):
        cols = ds(k, 256)
        acc = fg_p[d, :, cols].astype(F32)
        for j in range(1, 8):
            acc = acc + fg_r[(d + j) % 8, :, cols].astype(F32)
        fg_out[cols, :] = acc.T.astype(BF)
        return 0

    lax.fori_loop(0, DB // 256, fg_sum, 0)

    for s in range(2):
        arrived(sg_out.at[:, s * CB : (s + 1) * CB], c8_rs.at[s])

    for cp in sends:
        cp.wait_send()
    for k in range(1, 4):
        og_copies[k].wait_send()

    @pl.when(jnp.logical_not(og_self))
    def _():
        og_copies[0].wait_send()

    for s in range(2):

        @pl.when(jnp.logical_not(is_me(c8_to[s])))
        def _(s=s):
            c8_copies[s].wait_send()

        for k in range(1, 4):
            cols = slice(s * CB, (s + 1) * CB)
            q = (z + k) % 4
            remote(
                sg_p.at[q, :, cols], sg_r.at[z, :, cols], sg_ss.at[k * 2 + s], sg_rs.at[z * 2 + s], dev(x, y, q, c)
            ).wait_send()
    for k in range(1, 8):
        to = (d + k) % 8
        remote(fg_p.at[to], fg_r.at[d], fg_ss.at[k - 1], fg_rs.at[d], (to, f)).wait_send()
    for k in range(1, 4):
        to = (x + k) % 4
        remote(ig_p.at[to], ig_r.at[x], ig_ss.at[k - 1], ig_rs.at[x], dev(to, y, z, c)).wait_send()


def shards(inputs, first_factor, second_factor, out_grad):
    ff = first_factor.reshape(4, 4, FB, RK)
    any_ = pl.BlockSpec(memory_space=pl.ANY)
    vmem = pl.BlockSpec(memory_space=pltpu.VMEM)
    dma = pltpu.SemaphoreType.DMA
    return pl.pallas_call(
        kernel,
        name="backward",
        out_shape=(
            jax.ShapeDtypeStruct((TOK, FB), BF),
            jax.ShapeDtypeStruct((DB, RK), BF),
            jax.ShapeDtypeStruct((RK, 2 * CB), BF),
        ),
        in_specs=[any_] * 4,
        out_specs=(vmem, vmem, vmem),
        scratch_shapes=[
            pltpu.VMEM((TOK, D), BF),
            pltpu.VMEM((4, 4, FB, RK), BF),
            pltpu.VMEM((2 * TOK, 2 * CB), BF),
            pltpu.VMEM((4 * RK, 2 * CB), BF),
            pltpu.VMEM((4, FB, 4 * RK), BF),
            pltpu.VMEM((4 * RK, 2 * TOK), BF),
            pltpu.VMEM((TOK, RK), F32),
            pltpu.VMEM((2, 2, TOK, 256), F32),
            pltpu.VMEM((2, TOK, 4 * RK), BF),
            pltpu.VMEM((8, TOK, RK), BF),
            pltpu.VMEM((TOK, 4 * RK), BF),
            pltpu.VMEM((4, RK, 2 * CB), BF),
            pltpu.VMEM((4, RK, 2 * CB), BF),
            pltpu.VMEM((RK, 2 * CB), BF),
            pltpu.VMEM((8, RK, DB), BF),
            pltpu.VMEM((8, RK, DB), BF),
            pltpu.VMEM((4, TOK, FB), BF),
            pltpu.VMEM((4, TOK, FB), BF),
            pltpu.VMEM((RK, TOK), BF),
            dma((4,)), dma((4,)),
            dma((4,)), dma((4,)),
            dma((6,)), dma((8,)),
            dma((3,)), dma((4,)),
            dma((8,)), dma((8,)),
            dma((8,)), dma((8,)),
            dma((3,)), dma((4,)),
            dma((8,)), dma((8,)),
            dma((2,)), dma((2,)),
            dma((7,)), dma((8,)),
            dma((3,)), dma((4,)),
        ],
        cost_estimate=pl.CostEstimate(flops=10_100_000_000, bytes_accessed=30_000_000, transcendentals=0),
        compiler_params=pltpu.CompilerParams(
            collective_id=0, has_side_effects=True, vmem_limit_bytes=63 * 1024 * 1024
        ),
    )(inputs, ff, second_factor, out_grad)


def solution(mesh):
    in_specs = (P("dp", None), P(None, "factor"), P("factor", None), P("dp", "factor"))
    out_specs = (P("dp", "factor"), P("dp", "factor"), P("factor", "dp"))
    return jax.shard_map(shards, mesh=mesh, in_specs=in_specs, out_specs=out_specs, check_vma=False)
```

```python
import functools

import jax
import jax.numpy as jnp
from jax import lax
from jax.experimental import pallas as pl
from jax.experimental.pallas import tpu as pltpu
from jax.sharding import PartitionSpec as P

MESH = pl.DeviceIdType.MESH
BF = jnp.bfloat16
F32 = jnp.float32
TOK = 384
D = 16384
RK = 128
CB = 1664
FB = 1024
DB = 2048


def ds(i, n):
    return pl.ds(pl.multiple_of(i * n, n), n)


def nn(a, b):
    return jnp.dot(a, b, preferred_element_type=F32)


def nt(a, b):
    return lax.dot_general(a, b, (((1,), (1,)), ((), ())), preferred_element_type=F32)


def kernel(
    inp, ff, sf, og,
    ig_out, fg_out, sg_out,
    i_v, ff_v, og_r, sf_r, ffx, ht, h_acc, rg_acc, rg_p, rg_r, rg_all,
    sg_p, sg_r, sg_s, fg_p, fg_y, fg_z, fg_f, ig_p, ig_r, rgt,
    i_sem, ff_sem,
    og_ss, og_rs, fwd_ss, sf_ss, sf_rs, fx_ss, fx_rs, h_ss, h_rs, rg_ss, rg_rs, ra_ss, ra_rs,
    sg_ss, sg_rs, c8_ss, c8_rs, fy_ss, fy_rs, fz_ss, fz_rs, ff_ss, ff_rs, ig_ss, ig_rs,
):
    d = lax.axis_index("dp")
    f = lax.axis_index("factor")
    yl, z = d // 4, d % 4
    x, yh, c = f // 4, (f // 2) % 2, f % 2
    y = 2 * yh + yl
    yp = 2 * yh + 1 - yl
    r4 = yh * 2 + c
    line = y * 2 + c
    root = c == x % 2
    s0, s1 = x // 2, 1 - x // 2

    def dev(x_, y_, z_, c_):
        return ((y_ % 2) * 4 + z_, x_ * 4 + (y_ // 2) * 2 + c_)

    def remote(src, dst, ss, rs, to):
        return pltpu.make_async_remote_copy(
            src_ref=src, dst_ref=dst, send_sem=ss, recv_sem=rs, device_id=to, device_id_type=MESH
        )

    def arrived(dst, rs):
        pltpu.make_async_copy(dst, dst, rs).wait()

    sends = []

    def send(cp, cond=None):
        if cond is None:
            cp.start()
        else:
            pl.when(cond)(cp.start)
        sends.append((cond, cp))

    c8_to = [(x, 2 * (z // 2) + s, 2 * c + yh, z % 2) for s in range(2)]
    c8_from = [(x, 2 * (z % 2) + s, 2 * yh + c, z // 2) for s in range(2)]

    def is_me(t):
        return (t[1] == y) & (t[2] == z) & (t[3] == c)

    barrier = pltpu.get_barrier_semaphore()

    def greet(*t):
        pl.semaphore_signal(barrier, inc=1, device_id=dev(*t), device_id_type=MESH)

    for j in range(1, 8):
        other = (line + j) % 8
        greet(x, other // 2, z, other % 2)
    for k in range(1, 4):
        for cc in range(2):
            greet((x + k) % 4, y, z, cc)
    for k in range(1, 4):
        greet(x, y, (z + k) % 4, c)
    extra = 0
    for t in c8_to + c8_from:
        away = jnp.logical_not(is_me(t))

        @pl.when(away)
        def _(t=t):
            greet(*t)

        extra = extra + away.astype(jnp.int32)
    pl.semaphore_wait(barrier, 16 + extra)

    stays = c == yl
    moves = jnp.logical_not(stays)
    right, left = (x + 1) % 4, (x + 3) % 4
    og_dst = og_r.at[s0, ds(yl, TOK), :]
    og_rsem = og_rs.at[s0 * 2 + yl]
    send(remote(og, og_dst, og_ss.at[0], og_rsem, dev(right, y, z, x % 2)), stays)
    send(remote(og, og_dst, og_ss.at[1], og_rsem, dev(left, y, z, x % 2)), stays)
    send(remote(og, og_dst, og_ss.at[2], og_rsem, dev(x, yp, z, x % 2)), moves)
    send(remote(og, og_dst, og_ss.at[3], og_rsem, dev(x, y, z, 1 - c)), stays & jnp.logical_not(root))

    @pl.when(stays & root)
    def _():
        pltpu.make_async_copy(og, og_dst, og_rsem).start()

    ff_loads = [pltpu.make_async_copy(ff.at[k], ff_v.at[k], ff_sem.at[k]) for k in range(4)]
    i_loads = [
        pltpu.make_async_copy(inp.at[:, k * 4096 : (k + 1) * 4096], i_v.at[:, k * 4096 : (k + 1) * 4096], i_sem.at[k])
        for k in range(4)
    ]
    for k in range(4):
        ff_loads[k].start()
        i_loads[k].start()

    peers = [(y, 1 - c), (3 - y, 0), (3 - y, 1)]

    def sf_src(y_, c_, s):
        return sf.at[:, ds((2 * s + c_) * 4 + (y_ // 2) * 2 + y_ % 2, CB)]

    def sf_send(n, s):
        dst, rs = sf_r.at[s, ds(r4, RK), :], sf_rs.at[r4 * 2 + s]
        pltpu.make_async_copy(sf_src(y, c, s), dst, rs).start()
        for m, (y_, c_) in enumerate(peers):
            send(remote(sf_src(y_, c_, s), dst, sf_ss.at[m * 2 + n], rs, dev(x, y_, z, c_)))

    def fx_send(k):
        to = (x + k) % 4
        dst, rs = ffx.at[to, :, ds(r4, RK)], fx_rs.at[to * 4 + r4]
        pltpu.make_async_copy(ff.at[to, r4], dst, rs).start()
        for m, (y_, c_) in enumerate(peers):
            send(remote(ff.at[to, (y_ // 2) * 2 + c_], dst, fx_ss.at[m * 4 + k], rs, dev(x, y_, z, c_)))

    sf_send(0, s0)

    h_acc[...] = jnp.zeros_like(h_acc)
    for k in range(4):
        ff_loads[k].wait()
        i_loads[k].wait()

        def h_step(j, _, k=k):
            h_acc[...] += nn(i_v[:, ds(k * 4 + j, FB)], ff_v[k, j])
            return 0

        lax.fori_loop(0, 4, h_step, 0)
    ht_mine = ht.at[ds(r4, RK), ds(yl, TOK)]
    ht_mine[...] = h_acc[...].T.astype(BF)
    for j in range(1, 8):
        other = (line + j) % 8
        send(remote(ht_mine, ht_mine, h_ss.at[j], h_rs.at[line], dev(x, other // 2, z, other % 2)))

    sf_send(1, s1)
    fx_send(2)
    fx_send(1)

    rg_acc[...] = jnp.zeros_like(rg_acc)

    def sf_wait(s):
        for q in range(4):
            arrived(sf_r.at[s, q * RK : (q + 1) * RK, :], sf_rs.at[q * 2 + s])

    def block(s, t):
        arrived(og_r.at[s, ds(t, TOK), :], og_rs.at[s * 2 + t])

    def rg_block(s, t):
        def step(n, _):
            rg_acc[t, n] += nt(og_r[s, ds(t, TOK), :], sf_r[s, ds(n, 256), :])
            return 0

        lax.fori_loop(0, 2, step, 0)

    def sg_copy(k, s):
        q = (z + k) % 4
        return remote(sg_p.at[s, q], sg_r.at[s, z], sg_ss.at[k * 2 + s], sg_rs.at[z * 2 + s], dev(x, y, q, c))

    def sg_block(s):
        def step(i, _):
            k = (i + 2) % 4
            q = (z + k) % 4
            sg_p[s, q] = nn(ht[ds(q, RK), :], og_r[s]).astype(BF)

            @pl.when(k != 0)
            def _():
                sg_copy(k, s).start()

            return 0

        lax.fori_loop(0, 4, step, 0)

    def pick(u, v):
        return jnp.where(root, u, v)

    def onward(i, s, t):
        src = og_r.at[s, ds(t, TOK), :]
        from_left = (2 * s + c) == left
        mine = root & (s == s0) & (t != yl)
        ahead = jnp.logical_not(root) & (t == 0) & from_left
        back = jnp.logical_not(root) & (t == 1) & jnp.logical_not(from_left)
        rs = og_rs.at[s * 2 + t]
        send(remote(src, src, fwd_ss.at[i * 2], rs, dev(right, y, z, c)), mine | ahead)
        send(remote(src, src, fwd_ss.at[i * 2 + 1], rs, dev(left, y, z, c)), mine | back)

    order = [(s0, yl), (pick(s0, s1), pick(1 - yl, yl)), (pick(s1, s0), pick(yl, 1 - yl)), (s1, 1 - yl)]
    block(*order[0])
    onward(0, *order[0])
    block(*order[1])
    onward(1, *order[1])
    sf_wait(s0)
    rg_block(*order[0])
    sf_wait(s1)
    rg_block(*order[1])
    for j in range(1, 8):
        other = (line + j) % 8
        y_, c_ = other // 2, other % 2
        arrived(ht.at[ds((y_ // 2) * 2 + c_, RK), ds(y_ % 2, TOK)], h_rs.at[other])

    @pl.when(root)
    def _():
        sg_block(s0)

    block(*order[2])
    onward(2, *order[2])
    rg_block(*order[2])
    block(*order[3])
    onward(3, *order[3])
    rg_block(*order[3])

    for t in range(2):
        for n in range(2):
            rg_p[t, :, n * 256 : (n + 1) * 256] = rg_acc[t, n].astype(BF)
    for j in range(1, 8):
        other = (line + j) % 8
        y_, c_ = other // 2, other % 2
        send(
            remote(
                rg_p.at[y_ % 2, :, ds((y_ // 2) * 2 + c_, RK)], rg_r.at[line], rg_ss.at[j], rg_rs.at[line],
                dev(x, y_, z, c_),
            )
        )

    @pl.when(jnp.logical_not(root))
    def _():
        sg_block(s0)

    sg_block(s1)

    total = rg_p[yl, :, ds(r4, RK)].astype(F32)
    for j in range(1, 8):
        other = (line + j) % 8
        arrived(rg_r.at[other], rg_rs.at[other])
        total = total + rg_r[other].astype(F32)
    rg_mine = rg_all.at[:, ds(r4, RK)]
    rg_mine[...] = total.astype(BF)
    for n, (y_, c_) in enumerate([(y, 1 - c), ((y + 2) % 4, 0), ((y + 2) % 4, 1)]):
        send(remote(rg_mine, rg_mine, ra_ss.at[n], ra_rs.at[r4], dev(x, y_, z, c_)))
    rgt[...] = total.T.astype(BF)
    fx_send(3)
    fx_send(0)

    def fg_unit(own, z_, half):
        u = (pick_yl(own) * 4 + z_) * 2 + half
        fg_p[u] = nn(rgt[...], i_v[:, ds(u, FB)]).astype(BF)
        return u

    def pick_yl(own):
        return yl if own else 1 - yl

    def z_copy(kind, u, k):
        to = (z + k) % 4
        return remote(fg_p.at[u], fg_z.at[kind, z], fz_ss.at[kind * 4 + k], fz_rs.at[kind * 4 + z], dev(x, y, to, c))

    def y_copy(u, z_):
        return remote(fg_p.at[u], fg_y.at[z_], fy_ss.at[z_], fy_rs.at[z_], dev(x, yp, z, c))

    def p2(i, _):
        z_ = (z + i + 2) % 4
        y_copy(fg_unit(False, z_, 1), z_).start()
        return 0

    lax.fori_loop(0, 4, p2, 0)
    for own in (False, True):

        def first(i, _, own=own):
            k = (i + 2) % 4
            u = fg_unit(own, (z + k) % 4, 0)

            @pl.when(k != 0)
            def _():
                z_copy(0 if own else 1, u, k).start()

            return 0

        lax.fori_loop(0, 4, first, 0)

    def o2(z_, _):
        fg_unit(True, z_, 1)
        return 0

    lax.fori_loop(0, 4, o2, 0)

    for j in range(1, 4):
        other = (r4 + j) % 4
        arrived(rg_all.at[:, ds(other, RK)], ra_rs.at[other])

    def ig_copy(k):
        to = (x + k) % 4
        return remote(ig_p.at[to], ig_r.at[x], ig_ss.at[k], ig_rs.at[x], dev(to, y, z, c))

    def ig_part(k):
        to = (x + k) % 4
        for j in range(4):
            arrived(ffx.at[to, :, j * RK : (j + 1) * RK], fx_rs.at[to * 4 + j])
        ig_p[to] = nt(rg_all[...], ffx[to]).astype(BF)
        if k:
            send(ig_copy(k))

    ig_part(2)
    ig_part(1)

    def merge(i, _):
        k = (i + 2) % 4
        z_ = (z + k) % 4
        u = (yl * 4 + z_) * 2 + 1
        arrived(fg_y.at[z_], fy_rs.at[z_])
        fg_p[u] = (fg_p[u].astype(F32) + fg_y[z_].astype(F32)).astype(BF)

        @pl.when(k != 0)
        def _():
            z_copy(2, u, k).start()

        return 0

    lax.fori_loop(0, 4, merge, 0)
    ig_part(3)
    ig_part(0)

    for s in range(2):
        for j in range(1, 4):
            other = (z + j) % 4
            arrived(sg_r.at[s, other], sg_rs.at[other * 2 + s])
        total = sg_p[s, z].astype(F32)
        for j in range(1, 4):
            total = total + sg_r[s, (z + j) % 4].astype(F32)
        sg_s[s] = total.astype(BF)
        dst = sg_out.at[:, ds(yl, CB)]
        near = pltpu.make_async_copy(sg_s.at[s], dst, c8_rs.at[yl])
        send(remote(sg_s.at[s], dst, c8_ss.at[s], c8_rs.at[yl], dev(*c8_to[s])), jnp.logical_not(is_me(c8_to[s])))
        pl.when(is_me(c8_to[s]))(near.start)

    for j in range(1, 4):
        other = (z + j) % 4
        arrived(fg_z.at[1, other], fz_rs.at[4 + other])
    total = fg_p[((1 - yl) * 4 + z) * 2].astype(F32)
    for j in range(1, 4):
        total = total + fg_z[1, (z + j) % 4].astype(F32)
    fg_f[0] = total.astype(BF)
    send(remote(fg_f.at[0], fg_f.at[1], ff_ss.at[0], ff_rs.at[0], dev(x, yp, z, c)))

    for j in range(1, 4):
        other = (x + j) % 4
        arrived(ig_r.at[other], ig_rs.at[other])

    def ig_sum(k, _):
        rows = ds(k, 64)
        acc = ig_p[x, rows, :].astype(F32)
        for j in range(1, 4):
            acc = acc + ig_r[(x + j) % 4, rows, :].astype(F32)
        ig_out[rows, :] = acc.astype(BF)
        return 0

    lax.fori_loop(0, TOK // 64, ig_sum, 0)

    for half in range(2):
        kind = 2 * half
        for j in range(1, 4):
            other = (z + j) % 4
            arrived(fg_z.at[kind, other], fz_rs.at[kind * 4 + other])
        if half == 0:
            arrived(fg_f.at[1], ff_rs.at[0])

        def fg_sum(k, _, half=half, kind=kind):
            cols = ds(k, 256)
            acc = fg_p[d * 2 + half, :, cols].astype(F32)
            for j in range(1, 4):
                acc = acc + fg_z[kind, (z + j) % 4, :, cols].astype(F32)
            if half == 0:
                acc = acc + fg_f[1, :, cols].astype(F32)
            fg_out[ds(half * 4 + k, 256), :] = acc.T.astype(BF)
            return 0

        lax.fori_loop(0, FB // 256, fg_sum, 0)

    for s in range(2):
        arrived(sg_out.at[:, s * CB : (s + 1) * CB], c8_rs.at[s])

    for cond, cp in sends:
        if cond is None:
            cp.wait_send()
        else:
            pl.when(cond)(cp.wait_send)
    for k in range(1, 4):
        for s in range(2):
            sg_copy(k, s).wait_send()
        z_ = (z + k) % 4
        z_copy(0, (yl * 4 + z_) * 2, k).wait_send()
        z_copy(1, ((1 - yl) * 4 + z_) * 2, k).wait_send()
        z_copy(2, (yl * 4 + z_) * 2 + 1, k).wait_send()
    for z_ in range(4):
        y_copy(((1 - yl) * 4 + z_) * 2 + 1, z_).wait_send()


def shards(inputs, first_factor, second_factor, out_grad):
    ff = first_factor.reshape(4, 4, FB, RK)
    any_ = pl.BlockSpec(memory_space=pl.ANY)
    vmem = pl.BlockSpec(memory_space=pltpu.VMEM)
    dma = pltpu.SemaphoreType.DMA
    return pl.pallas_call(
        kernel,
        name="backward",
        out_shape=(
            jax.ShapeDtypeStruct((TOK, FB), BF),
            jax.ShapeDtypeStruct((DB, RK), BF),
            jax.ShapeDtypeStruct((RK, 2 * CB), BF),
        ),
        in_specs=[any_] * 4,
        out_specs=(vmem, vmem, vmem),
        scratch_shapes=[
            pltpu.VMEM((TOK, D), BF),
            pltpu.VMEM((4, 4, FB, RK), BF),
            pltpu.VMEM((2, 2 * TOK, CB), BF),
            pltpu.VMEM((2, 4 * RK, CB), BF),
            pltpu.VMEM((4, FB, 4 * RK), BF),
            pltpu.VMEM((4 * RK, 2 * TOK), BF),
            pltpu.VMEM((TOK, RK), F32),
            pltpu.VMEM((2, 2, TOK, 256), F32),
            pltpu.VMEM((2, TOK, 4 * RK), BF),
            pltpu.VMEM((8, TOK, RK), BF),
            pltpu.VMEM((TOK, 4 * RK), BF),
            pltpu.VMEM((2, 4, RK, CB), BF),
            pltpu.VMEM((2, 4, RK, CB), BF),
            pltpu.VMEM((2, RK, CB), BF),
            pltpu.VMEM((16, RK, FB), BF),
            pltpu.VMEM((4, RK, FB), BF),
            pltpu.VMEM((3, 4, RK, FB), BF),
            pltpu.VMEM((2, RK, FB), BF),
            pltpu.VMEM((4, TOK, FB), BF),
            pltpu.VMEM((4, TOK, FB), BF),
            pltpu.VMEM((RK, TOK), BF),
            dma((4,)), dma((4,)),
            dma((4,)), dma((4,)), dma((8,)),
            dma((6,)), dma((8,)),
            dma((12,)), dma((16,)),
            dma((8,)), dma((8,)),
            dma((8,)), dma((8,)),
            dma((3,)), dma((4,)),
            dma((8,)), dma((8,)),
            dma((2,)), dma((2,)),
            dma((4,)), dma((4,)),
            dma((12,)), dma((12,)),
            dma((1,)), dma((1,)),
            dma((4,)), dma((4,)),
        ],
        cost_estimate=pl.CostEstimate(flops=10_100_000_000, bytes_accessed=30_000_000, transcendentals=0),
        compiler_params=pltpu.CompilerParams(
            collective_id=0, has_side_effects=True, vmem_limit_bytes=63 * 1024 * 1024
        ),
    )(inputs, ff, second_factor, out_grad)


def solution(mesh):
    in_specs = (P("dp", None), P(None, "factor"), P("factor", None), P("dp", "factor"))
    out_specs = (P("dp", "factor"), P("dp", "factor"), P("factor", "dp"))
    return jax.shard_map(shards, mesh=mesh, in_specs=in_specs, out_specs=out_specs, check_vma=False)
```

```python
import functools

import jax
import jax.numpy as jnp
from jax import lax
from jax.experimental import pallas as pl
from jax.experimental.pallas import tpu as pltpu
from jax.sharding import PartitionSpec as P

MESH = pl.DeviceIdType.MESH
BF = jnp.bfloat16
F32 = jnp.float32
TOK = 384
D = 16384
RK = 128
QR = 32
CB = 1664
FB = 1024
DB = 2048


def ds(i, n):
    return pl.ds(pl.multiple_of(i * n, n), n)


def nn(a, b):
    return jnp.dot(a, b, preferred_element_type=F32)


def nt(a, b):
    return lax.dot_general(a, b, (((1,), (1,)), ((), ())), preferred_element_type=F32)


def kernel(
    inp, ff, sf, og,
    ig_out, fg_out, sg_out,
    i_v, ff_v, og_r, sf_r, ffx, ht, h_acc, rg_acc, rg_p, rg_r, rg_all,
    sg_p, sg_m, sg_r, sg_s, fg_p, fg_y, fg_m, fg_z, fg_f, ig_p, ig_m, ig_r, rgt,
    i_sem, ff_sem,
    og_ss, og_rs, fwd_ss, sf_ss, sf_rs, sq_rs, fx_ss, fx_rs, fxh_rs, h_ss, h_rs, rg_ss, rg_rs, ra_ss, ra_rs,
    sg_ss, sg_rs, c8_ss, c8_rs, fy_ss, fy_rs, fz_ss, fz_rs, ff_ss, ff_rs, ig_ss, ig_rs,
):
    d = lax.axis_index("dp")
    f = lax.axis_index("factor")
    yl, z = d // 4, d % 4
    x, yh, c = f // 4, (f // 2) % 2, f % 2
    y = 2 * yh + yl
    yp = 2 * yh + 1 - yl
    r4 = yh * 2 + c
    line = y * 2 + c
    root = c == x % 2
    s0, s1 = x // 2, 1 - x // 2

    def dev(x_, y_, z_, c_):
        return ((y_ % 2) * 4 + z_, x_ * 4 + (y_ // 2) * 2 + c_)

    def remote(src, dst, ss, rs, to):
        return pltpu.make_async_remote_copy(
            src_ref=src, dst_ref=dst, send_sem=ss, recv_sem=rs, device_id=to, device_id_type=MESH
        )

    def arrived(dst, rs):
        pltpu.make_async_copy(dst, dst, rs).wait()

    sends = []

    def send(cp, cond=None):
        if cond is None:
            cp.start()
        else:
            pl.when(cond)(cp.start)
        sends.append((cond, cp))

    class RingSum:
        def __init__(self, at, to_dev, part, rows, mid, out, ss, rs, base):
            far, up, down = (at + 2) % 4, (at + 1) % 4, (at + 3) % 4
            lo, hi = pl.ds(0, rows // 2), pl.ds(rows // 2, rows // 2)

            def cp(n, src, dst, to):
                return remote(src, dst, ss.at[base + n], rs.at[base + n], to_dev(to))

            self.mid = mid
            self.far = [cp(0, part(far).at[lo], mid.at[0], up), cp(1, part(far).at[hi], mid.at[1], down)]
            self.plain = [cp(2, part(up).at[hi], out.at[0, hi], up), cp(3, part(down).at[lo], out.at[1, lo], down)]
            self.merged = [cp(4, part(up).at[lo], out.at[0, lo], up), cp(5, part(down).at[hi], out.at[1, hi], down)]
            self.own = [part(up).at[lo], part(down).at[hi]]
            self.mids = [(mid.at[0], rs.at[base]), (mid.at[1], rs.at[base + 1])]
            self.outs = [
                (out.at[0, hi], rs.at[base + 2]), (out.at[1, lo], rs.at[base + 3]),
                (out.at[0, lo], rs.at[base + 4]), (out.at[1, hi], rs.at[base + 5]),
            ]

        def part_done(self, i):
            pl.when(i == 0)(self.send_far)
            pl.when(i == 1)(self.plain[1].start)
            pl.when(i == 2)(self.plain[0].start)

        def send_far(self):
            self.far[0].start()
            self.far[1].start()

        def merge(self):
            for n, own in enumerate(self.own):
                arrived(*self.mids[n])
                own[...] = (own[...].astype(F32) + self.mid[n].astype(F32)).astype(BF)
                self.merged[n].start()

        def wait(self):
            for ref, sem in self.outs:
                arrived(ref, sem)

        def drain(self):
            for cp in self.far + self.plain + self.merged:
                cp.wait_send()

    def steps(i):
        return jnp.where(i < 2, i + 2, 3 - i)

    def z_dev(to):
        return dev(x, y, to, c)

    c8_to = [(x, 2 * (z // 2) + s, 2 * c + yh, z % 2) for s in range(2)]
    c8_from = [(x, 2 * (z % 2) + s, 2 * yh + c, z // 2) for s in range(2)]

    def is_me(t):
        return (t[1] == y) & (t[2] == z) & (t[3] == c)

    barrier = pltpu.get_barrier_semaphore()

    def greet(*t):
        pl.semaphore_signal(barrier, inc=1, device_id=dev(*t), device_id_type=MESH)

    for j in range(1, 8):
        other = (line + j) % 8
        greet(x, other // 2, z, other % 2)
    for k in range(1, 4):
        for cc in range(2):
            greet((x + k) % 4, y, z, cc)
    for k in range(1, 4):
        greet(x, y, (z + k) % 4, c)
    extra = 0
    for t in c8_to + c8_from:
        away = jnp.logical_not(is_me(t))

        @pl.when(away)
        def _(t=t):
            greet(*t)

        extra = extra + away.astype(jnp.int32)
    pl.semaphore_wait(barrier, 16 + extra)

    stays = c == yl
    moves = jnp.logical_not(stays)
    right, left = (x + 1) % 4, (x + 3) % 4
    og_dst = og_r.at[s0, ds(yl, TOK), :]
    og_rsem = og_rs.at[s0 * 2 + yl]
    send(remote(og, og_dst, og_ss.at[0], og_rsem, dev(right, y, z, x % 2)), stays)
    send(remote(og, og_dst, og_ss.at[1], og_rsem, dev(left, y, z, x % 2)), stays)
    send(remote(og, og_dst, og_ss.at[2], og_rsem, dev(x, yp, z, x % 2)), moves)
    send(remote(og, og_dst, og_ss.at[3], og_rsem, dev(x, y, z, 1 - c)), stays & jnp.logical_not(root))

    @pl.when(stays & root)
    def _():
        pltpu.make_async_copy(og, og_dst, og_rsem).start()

    ff_loads = [pltpu.make_async_copy(ff.at[k], ff_v.at[k], ff_sem.at[k]) for k in range(4)]
    i_loads = [
        pltpu.make_async_copy(inp.at[:, k * 4096 : (k + 1) * 4096], i_v.at[:, k * 4096 : (k + 1) * 4096], i_sem.at[k])
        for k in range(4)
    ]
    for k in range(4):
        ff_loads[k].start()
        i_loads[k].start()

    peers = [(y, 1 - c), (3 - y, 0), (3 - y, 1)]

    def sf_src(y_, c_, s):
        return sf.at[:, ds((2 * s + c_) * 4 + (y_ // 2) * 2 + y_ % 2, CB)]

    def sf_row(s, r, q):
        return sf_r.at[s, pl.ds(pl.multiple_of(r * RK + q * QR, QR), QR), :]

    for n, s in enumerate((s0, s1)):
        dst, rs = sf_r.at[s, ds(r4, RK), :], sf_rs.at[r4 * 2 + s]
        pltpu.make_async_copy(sf_src(y, c, s), dst, rs).start()
        send(remote(sf_src(y, 1 - c, s), dst, sf_ss.at[n], rs, dev(x, y, z, 1 - c)))
    for m, (y_, c_) in enumerate(peers[1:]):
        src = sf_src(y_, c_, s0).at[ds(z, QR), :]
        send(remote(src, sf_row(s0, r4, z), sf_ss.at[2 + m], sq_rs.at[r4 * 4 + z], dev(x, y_, z, c_)))

    def sf_far():
        for m, (y_, c_) in enumerate(peers[1:]):
            dst, rs = sf_r.at[s1, ds(r4, RK), :], sf_rs.at[r4 * 2 + s1]
            send(remote(sf_src(y_, c_, s1), dst, sf_ss.at[4 + m], rs, dev(x, y_, z, c_)))

    def sf_onward():
        for m in range(2):
            r = (1 - yh) * 2 + m
            unit, rs = sf_row(s0, r, z), sq_rs.at[r * 4 + z]
            arrived(unit, rs)
            for k in (2, 1, 3):
                send(remote(unit, unit, sf_ss.at[6 + m * 3 + k - 1], rs, z_dev((z + k) % 4)))

    def sf_wait_s0():
        for m in range(2):
            r = yh * 2 + m
            arrived(sf_r.at[s0, ds(r, RK), :], sf_rs.at[r * 2 + s0])
            r = (1 - yh) * 2 + m
            for k in range(1, 4):
                q = (z + k) % 4
                arrived(sf_row(s0, r, q), sq_rs.at[r * 4 + q])

    for k in range(4):
        dst = ffx.at[k, :, ds(r4, RK)]
        pltpu.make_async_copy(ff.at[k, r4], dst, fx_rs.at[k * 4 + r4]).start()
        send(remote(ff.at[k, yh * 2 + 1 - c], dst, fx_ss.at[k], fx_rs.at[k * 4 + r4], dev(x, y, z, 1 - c)))
    x_far = (x + 2 + z % 2) % 4

    def fx_half(to, h, r):
        return ffx.at[to, ds(h, FB // 2), ds(r, RK)]

    for m, (y_, c_) in enumerate(peers[1:]):
        src = ff.at[x_far, (y_ // 2) * 2 + c_, ds(z // 2, FB // 2)]
        send(remote(src, fx_half(x_far, z // 2, r4), fx_ss.at[4 + m], fxh_rs.at[z * 4 + r4], dev(x, y_, z, c_)))

    def fx_onward():
        for m in range(2):
            r = (1 - yh) * 2 + m
            unit, rs = fx_half(x_far, z // 2, r), fxh_rs.at[z * 4 + r]
            arrived(unit, rs)
            for k in (2, 1, 3):
                send(remote(unit, unit, fx_ss.at[6 + m * 3 + k - 1], rs, z_dev((z + k) % 4)))

    def fx_near(k):
        to = (x + k) % 4
        for m, (y_, c_) in enumerate(peers[1:]):
            dst, rs = ffx.at[to, :, ds(r4, RK)], fx_rs.at[to * 4 + r4]
            send(remote(ff.at[to, (y_ // 2) * 2 + c_], dst, fx_ss.at[12 + k * 2 + m], rs, dev(x, y_, z, c_)))

    h_acc[...] = jnp.zeros_like(h_acc)
    for k in range(4):
        ff_loads[k].wait()
        i_loads[k].wait()

        def h_step(j, _, k=k):
            h_acc[...] += nn(i_v[:, ds(k * 4 + j, FB)], ff_v[k, j])
            return 0

        lax.fori_loop(0, 4, h_step, 0)
    ht_mine = ht.at[ds(r4, RK), ds(yl, TOK)]
    ht_mine[...] = h_acc[...].T.astype(BF)
    for j in range(1, 8):
        other = (line + j) % 8
        send(remote(ht_mine, ht_mine, h_ss.at[j], h_rs.at[line], dev(x, other // 2, z, other % 2)))

    sf_far()
    sf_onward()
    fx_near(1)

    rg_acc[...] = jnp.zeros_like(rg_acc)

    def sf_wait(s):
        for q in range(4):
            arrived(sf_r.at[s, q * RK : (q + 1) * RK, :], sf_rs.at[q * 2 + s])

    def block(s, t):
        arrived(og_r.at[s, ds(t, TOK), :], og_rs.at[s * 2 + t])

    def rg_block(s, t):
        def step(n, _):
            rg_acc[t, n] += nt(og_r[s, ds(t, TOK), :], sf_r[s, ds(n, 256), :])
            return 0

        lax.fori_loop(0, 2, step, 0)

    sgs = {}
    for name, s in (("s0", s0), ("s1", s1)):
        sgs[name] = RingSum(z, z_dev, lambda q, s=s: sg_p.at[s, q], RK, sg_m.at[s], sg_r.at[s], sg_ss, sg_rs, s * 6)

    def sg_block(name, s):
        def step(i, _):
            q = (z + steps(i)) % 4
            sg_p[s, q] = nn(ht[ds(q, RK), :], og_r[s]).astype(BF)
            sgs[name].part_done(i)
            return 0

        lax.fori_loop(0, 4, step, 0)

    def pick(u, v):
        return jnp.where(root, u, v)

    def onward(i, s, t):
        src = og_r.at[s, ds(t, TOK), :]
        from_left = (2 * s + c) == left
        mine = root & (s == s0) & (t != yl)
        ahead = jnp.logical_not(root) & (t == 0) & from_left
        back = jnp.logical_not(root) & (t == 1) & jnp.logical_not(from_left)
        rs = og_rs.at[s * 2 + t]
        send(remote(src, src, fwd_ss.at[i * 2], rs, dev(right, y, z, c)), mine | ahead)
        send(remote(src, src, fwd_ss.at[i * 2 + 1], rs, dev(left, y, z, c)), mine | back)

    order = [(s0, yl), (pick(s0, s1), pick(1 - yl, yl)), (pick(s1, s0), pick(yl, 1 - yl)), (s1, 1 - yl)]
    block(*order[0])
    onward(0, *order[0])
    block(*order[1])
    onward(1, *order[1])
    fx_onward()
    sf_wait_s0()
    rg_block(*order[0])
    for j in range(1, 8):
        other = (line + j) % 8
        y_, c_ = other // 2, other % 2
        arrived(ht.at[ds((y_ // 2) * 2 + c_, RK), ds(y_ % 2, TOK)], h_rs.at[other])

    @pl.when(root)
    def _():
        sg_block("s0", s0)

    block(*order[2])
    onward(2, *order[2])
    rg_block(s0, 1 - yl)

    @pl.when(jnp.logical_not(root))
    def _():
        sg_block("s0", s0)

    sgs["s0"].merge()
    block(*order[3])
    onward(3, *order[3])
    sf_wait(s1)
    rg_block(s1, yl)
    rg_block(s1, 1 - yl)

    for t in range(2):
        for n in range(2):
            rg_p[t, :, n * 256 : (n + 1) * 256] = rg_acc[t, n].astype(BF)
    for j in range(1, 8):
        other = (line + j) % 8
        y_, c_ = other // 2, other % 2
        send(
            remote(
                rg_p.at[y_ % 2, :, ds((y_ // 2) * 2 + c_, RK)], rg_r.at[line], rg_ss.at[j], rg_rs.at[line],
                dev(x, y_, z, c_),
            )
        )

    fx_near(0)
    sg_block("s1", s1)

    total = rg_p[yl, :, ds(r4, RK)].astype(F32)
    for j in range(1, 8):
        other = (line + j) % 8
        arrived(rg_r.at[other], rg_rs.at[other])
        total = total + rg_r[other].astype(F32)
    rg_mine = rg_all.at[:, ds(r4, RK)]
    rg_mine[...] = total.astype(BF)
    for n, (y_, c_) in enumerate([(y, 1 - c), ((y + 2) % 4, 0), ((y + 2) % 4, 1)]):
        send(remote(rg_mine, rg_mine, ra_ss.at[n], ra_rs.at[r4], dev(x, y_, z, c_)))
    rgt[...] = total.T.astype(BF)

    def fg_unit(own, z_, half):
        u = (pick_yl(own) * 4 + z_) * 2 + half
        fg_p[u] = nn(rgt[...], i_v[:, ds(u, FB)]).astype(BF)
        return u

    def pick_yl(own):
        return yl if own else 1 - yl

    fgs = [
        RingSum(
            z, z_dev, lambda z_, n=n, o=o: fg_p.at[(pick_yl(o) * 4 + z_) * 2 + n // 2], RK,
            fg_m.at[n], fg_z.at[n], fz_ss, fz_rs, n * 6,
        )
        for n, o in ((0, True), (1, False), (2, True))
    ]

    def y_copy(u, z_):
        return remote(fg_p.at[u], fg_y.at[z_], fy_ss.at[z_], fy_rs.at[z_], dev(x, yp, z, c))

    def p2(i, _):
        z_ = (z + i + 2) % 4
        y_copy(fg_unit(False, z_, 1), z_).start()
        return 0

    lax.fori_loop(0, 4, p2, 0)
    for own in (False, True):
        zs = fgs[0 if own else 1]

        def first(i, _, own=own, zs=zs):
            fg_unit(own, (z + steps(i)) % 4, 0)
            zs.part_done(i)
            return 0

        lax.fori_loop(0, 4, first, 0)
    sgs["s1"].merge()

    def o2(z_, _):
        fg_unit(True, z_, 1)
        return 0

    lax.fori_loop(0, 4, o2, 0)

    for j in range(1, 4):
        other = (r4 + j) % 4
        arrived(rg_all.at[:, ds(other, RK)], ra_rs.at[other])

    igs = RingSum(x, lambda to: dev(to, y, z, c), lambda x_: ig_p.at[x_], TOK, ig_m, ig_r, ig_ss, ig_rs, 0)

    def ig_part(i, _):
        to = (x + steps(i)) % 4
        for j in range(4):

            @pl.when((i >= 2) | (j // 2 == yh))
            def _(j=j):
                arrived(ffx.at[to, :, j * RK : (j + 1) * RK], fx_rs.at[to * 4 + j])

            for h in range(2):

                @pl.when((i < 2) & (j // 2 != yh) & (i + 2 * h != z))
                def _(j=j, h=h):
                    arrived(fx_half(to, h, j), fxh_rs.at[(i + 2 * h) * 4 + j])

        ig_p[to] = nt(rg_all[...], ffx[to]).astype(BF)
        igs.part_done(i)
        return 0

    lax.fori_loop(0, 4, ig_part, 0)
    fgs[1].merge()
    fgs[0].merge()
    igs.merge()

    for zs in sgs.values():
        zs.wait()
    for s in range(2):
        sg_s[s] = (sg_p[s, z].astype(F32) + sg_r[s, 0].astype(F32) + sg_r[s, 1].astype(F32)).astype(BF)
        dst = sg_out.at[:, ds(yl, CB)]
        near = pltpu.make_async_copy(sg_s.at[s], dst, c8_rs.at[yl])
        send(remote(sg_s.at[s], dst, c8_ss.at[s], c8_rs.at[yl], dev(*c8_to[s])), jnp.logical_not(is_me(c8_to[s])))
        pl.when(is_me(c8_to[s]))(near.start)

    def merge(i, _):
        z_ = (z + steps(i)) % 4
        u = (yl * 4 + z_) * 2 + 1
        arrived(fg_y.at[z_], fy_rs.at[z_])
        fg_p[u] = (fg_p[u].astype(F32) + fg_y[z_].astype(F32)).astype(BF)
        fgs[2].part_done(i)
        return 0

    lax.fori_loop(0, 4, merge, 0)

    fgs[1].wait()
    total = fg_p[((1 - yl) * 4 + z) * 2].astype(F32) + fg_z[1, 0].astype(F32) + fg_z[1, 1].astype(F32)
    fg_f[0] = total.astype(BF)
    send(remote(fg_f.at[0], fg_f.at[1], ff_ss.at[0], ff_rs.at[0], dev(x, yp, z, c)))
    fgs[2].merge()


    igs.wait()

    def ig_sum(k, _):
        rows = ds(k, 64)
        acc = ig_p[x, rows, :].astype(F32) + ig_r[0, rows, :].astype(F32) + ig_r[1, rows, :].astype(F32)
        ig_out[rows, :] = acc.astype(BF)
        return 0

    lax.fori_loop(0, TOK // 64, ig_sum, 0)

    for half in range(2):
        kind = 2 * half
        fgs[kind].wait()
        if half == 0:
            arrived(fg_f.at[1], ff_rs.at[0])

        def fg_sum(k, _, half=half, kind=kind):
            cols = ds(k, 256)
            acc = fg_p[d * 2 + half, :, cols].astype(F32)
            for j in range(2):
                acc = acc + fg_z[kind, j, :, cols].astype(F32)
            if half == 0:
                acc = acc + fg_f[1, :, cols].astype(F32)
            fg_out[ds(half * 4 + k, 256), :] = acc.T.astype(BF)
            return 0

        lax.fori_loop(0, FB // 256, fg_sum, 0)

    for s in range(2):
        arrived(sg_out.at[:, s * CB : (s + 1) * CB], c8_rs.at[s])

    for cond, cp in sends:
        if cond is None:
            cp.wait_send()
        else:
            pl.when(cond)(cp.wait_send)
    for zs in list(sgs.values()) + fgs + [igs]:
        zs.drain()
    for z_ in range(4):
        y_copy(((1 - yl) * 4 + z_) * 2 + 1, z_).wait_send()


def place(a, b, c, a_out, b_out, c_out):
    a_out[...] = a[...]
    b_out[...] = b[...]
    c_out[...] = c[...]


def shards(inputs, first_factor, second_factor, out_grad):
    ff = first_factor.reshape(4, 4, FB, RK)
    any_ = pl.BlockSpec(memory_space=pl.ANY)
    vmem = pl.BlockSpec(memory_space=pltpu.VMEM)
    dma = pltpu.SemaphoreType.DMA
    results = pl.pallas_call(
        kernel,
        name="backward",
        out_shape=(
            jax.ShapeDtypeStruct((TOK, FB), BF),
            jax.ShapeDtypeStruct((DB, RK), BF),
            jax.ShapeDtypeStruct((RK, 2 * CB), BF),
        ),
        in_specs=[any_] * 4,
        out_specs=(vmem, vmem, vmem),
        scratch_shapes=[
            pltpu.VMEM((TOK, D), BF),
            pltpu.VMEM((4, 4, FB, RK), BF),
            pltpu.VMEM((2, 2 * TOK, CB), BF),
            pltpu.VMEM((2, 4 * RK, CB), BF),
            pltpu.VMEM((4, FB, 4 * RK), BF),
            pltpu.VMEM((4 * RK, 2 * TOK), BF),
            pltpu.VMEM((TOK, RK), F32),
            pltpu.VMEM((2, 2, TOK, 256), F32),
            pltpu.VMEM((2, TOK, 4 * RK), BF),
            pltpu.VMEM((8, TOK, RK), BF),
            pltpu.VMEM((TOK, 4 * RK), BF),
            pltpu.VMEM((2, 4, RK, CB), BF),
            pltpu.VMEM((2, 2, RK // 2, CB), BF),
            pltpu.VMEM((2, 2, RK, CB), BF),
            pltpu.VMEM((2, RK, CB), BF),
            pltpu.VMEM((16, RK, FB), BF),
            pltpu.VMEM((4, RK, FB), BF),
            pltpu.VMEM((3, 2, RK // 2, FB), BF),
            pltpu.VMEM((3, 2, RK, FB), BF),
            pltpu.VMEM((2, RK, FB), BF),
            pltpu.VMEM((4, TOK, FB), BF),
            pltpu.VMEM((2, TOK // 2, FB), BF),
            pltpu.VMEM((2, TOK, FB), BF),
            pltpu.VMEM((RK, TOK), BF),
            dma((4,)), dma((4,)),
            dma((4,)), dma((4,)), dma((8,)),
            dma((12,)), dma((8,)), dma((16,)),
            dma((16,)), dma((16,)), dma((16,)),
            dma((8,)), dma((8,)),
            dma((8,)), dma((8,)),
            dma((3,)), dma((4,)),
            dma((12,)), dma((12,)),
            dma((2,)), dma((2,)),
            dma((4,)), dma((4,)),
            dma((18,)), dma((18,)),
            dma((1,)), dma((1,)),
            dma((6,)), dma((6,)),
        ],
        cost_estimate=pl.CostEstimate(flops=10_100_000_000, bytes_accessed=30_000_000, transcendentals=0),
        compiler_params=pltpu.CompilerParams(
            collective_id=0, has_side_effects=True, vmem_limit_bytes=63 * 1024 * 1024
        ),
    )(inputs, ff, second_factor, out_grad)
    return pl.pallas_call(
        place,
        name="place",
        out_shape=[jax.ShapeDtypeStruct(r.shape, r.dtype) for r in results],
        in_specs=[vmem] * 3,
        out_specs=[vmem] * 3,
    )(*results)


def solution(mesh):
    in_specs = (P("dp", None), P(None, "factor"), P("factor", None), P("dp", "factor"))
    out_specs = (P("dp", "factor"), P("dp", "factor"), P("factor", "dp"))
    return jax.shard_map(shards, mesh=mesh, in_specs=in_specs, out_specs=out_specs, check_vma=False)
```

```python
import functools

import jax
import jax.numpy as jnp
from jax import lax
from jax.experimental import pallas as pl
from jax.experimental.pallas import tpu as pltpu
from jax.sharding import PartitionSpec as P

MESH = pl.DeviceIdType.MESH
BF = jnp.bfloat16
F32 = jnp.float32
TOK = 384
D = 16384
RK = 128
QR = 32
CB = 1664
FB = 1024
DB = 2048


def ds(i, n):
    return pl.ds(pl.multiple_of(i * n, n), n)


def nn(a, b):
    return jnp.dot(a, b, preferred_element_type=F32)


def nt(a, b):
    return lax.dot_general(a, b, (((1,), (1,)), ((), ())), preferred_element_type=F32)


def kernel(
    inp, ff, sf, og,
    ig_out, fg_out, sg_out,
    i_v, ff_v, og_r, sf_r, ffx, ht, h_acc, rg_acc, rg_p, rg_r, rg_all,
    sg_p, sg_m, sg_r, sg_s, fg_p, fg_y, fg_m, fg_z, fg_f, ig_p, ig_m, ig_r, rgt,
    i_sem, ff_sem,
    og_ss, og_rs, fwd_ss, sf_ss, sf_rs, sq_rs, fx_ss, fx_rs, fxh_rs, h_ss, h_rs, rg_ss, rg_rs, ra_ss, ra_rs,
    sg_ss, sg_rs, c8_ss, c8_rs, fy_ss, fy_rs, fz_ss, fz_rs, ff_ss, ff_rs, ig_ss, ig_rs,
):
    d = lax.axis_index("dp")
    f = lax.axis_index("factor")
    yl, z = d // 4, d % 4
    x, yh, c = f // 4, (f // 2) % 2, f % 2
    y = 2 * yh + yl
    yp = 2 * yh + 1 - yl
    r4 = yh * 2 + c
    line = y * 2 + c
    root = c == x % 2
    s0, s1 = x // 2, 1 - x // 2

    def dev(x_, y_, z_, c_):
        return ((y_ % 2) * 4 + z_, x_ * 4 + (y_ // 2) * 2 + c_)

    def remote(src, dst, ss, rs, to):
        return pltpu.make_async_remote_copy(
            src_ref=src, dst_ref=dst, send_sem=ss, recv_sem=rs, device_id=to, device_id_type=MESH
        )

    def arrived(dst, rs):
        pltpu.make_async_copy(dst, dst, rs).wait()

    sends = []

    def send(cp, cond=None):
        if cond is None:
            cp.start()
        else:
            pl.when(cond)(cp.start)
        sends.append((cond, cp))

    class RingSum:
        def __init__(self, at, to_dev, part, rows, mid, out, ss, rs, base):
            far, up, down = (at + 2) % 4, (at + 1) % 4, (at + 3) % 4
            lo, hi = pl.ds(0, rows // 2), pl.ds(rows // 2, rows // 2)

            def cp(n, src, dst, to):
                return remote(src, dst, ss.at[base + n], rs.at[base + n], to_dev(to))

            self.mid = mid
            self.far = [cp(0, part(far).at[lo], mid.at[0], up), cp(1, part(far).at[hi], mid.at[1], down)]
            self.plain = [cp(2, part(up).at[hi], out.at[0, hi], up), cp(3, part(down).at[lo], out.at[1, lo], down)]
            self.merged = [cp(4, part(up).at[lo], out.at[0, lo], up), cp(5, part(down).at[hi], out.at[1, hi], down)]
            self.own = [part(up).at[lo], part(down).at[hi]]
            self.mids = [(mid.at[0], rs.at[base]), (mid.at[1], rs.at[base + 1])]
            self.outs = [
                (out.at[0, hi], rs.at[base + 2]), (out.at[1, lo], rs.at[base + 3]),
                (out.at[0, lo], rs.at[base + 4]), (out.at[1, hi], rs.at[base + 5]),
            ]

        def part_done(self, i):
            pl.when(i == 0)(self.send_far)
            pl.when(i == 1)(self.plain[1].start)
            pl.when(i == 2)(self.plain[0].start)

        def send_far(self):
            self.far[0].start()
            self.far[1].start()

        def merge(self):
            for n, own in enumerate(self.own):
                arrived(*self.mids[n])
                own[...] = (own[...].astype(F32) + self.mid[n].astype(F32)).astype(BF)
                self.merged[n].start()

        def wait(self):
            for ref, sem in self.outs:
                arrived(ref, sem)

        def drain(self):
            for cp in self.far + self.plain + self.merged:
                cp.wait_send()

    def steps(i):
        return jnp.where(i < 2, i + 2, 3 - i)

    def z_dev(to):
        return dev(x, y, to, c)

    c8_to = [(x, 2 * (z // 2) + s, 2 * c + yh, z % 2) for s in range(2)]
    c8_from = [(x, 2 * (z % 2) + s, 2 * yh + c, z // 2) for s in range(2)]

    def is_me(t):
        return (t[1] == y) & (t[2] == z) & (t[3] == c)

    barrier = pltpu.get_barrier_semaphore()

    def greet(*t):
        pl.semaphore_signal(barrier, inc=1, device_id=dev(*t), device_id_type=MESH)

    for j in range(1, 8):
        other = (line + j) % 8
        greet(x, other // 2, z, other % 2)
    for k in range(1, 4):
        for cc in range(2):
            greet((x + k) % 4, y, z, cc)
    for k in range(1, 4):
        greet(x, y, (z + k) % 4, c)
    extra = 0
    for t in c8_to + c8_from:
        away = jnp.logical_not(is_me(t))

        @pl.when(away)
        def _(t=t):
            greet(*t)

        extra = extra + away.astype(jnp.int32)
    pl.semaphore_wait(barrier, 16 + extra)

    stays = c == yl
    moves = jnp.logical_not(stays)
    right, left = (x + 1) % 4, (x + 3) % 4
    og_dst = og_r.at[s0, ds(yl, TOK), :]
    og_rsem = og_rs.at[s0 * 2 + yl]
    send(remote(og, og_dst, og_ss.at[0], og_rsem, dev(right, y, z, x % 2)), stays)
    send(remote(og, og_dst, og_ss.at[1], og_rsem, dev(left, y, z, x % 2)), stays)
    send(remote(og, og_dst, og_ss.at[2], og_rsem, dev(x, yp, z, x % 2)), moves)
    send(remote(og, og_dst, og_ss.at[3], og_rsem, dev(x, y, z, 1 - c)), stays & jnp.logical_not(root))

    @pl.when(stays & root)
    def _():
        pltpu.make_async_copy(og, og_dst, og_rsem).start()

    ff_loads = [pltpu.make_async_copy(ff.at[k], ff_v.at[k], ff_sem.at[k]) for k in range(4)]
    i_loads = [
        pltpu.make_async_copy(inp.at[:, k * 4096 : (k + 1) * 4096], i_v.at[:, k * 4096 : (k + 1) * 4096], i_sem.at[k])
        for k in range(4)
    ]
    for k in range(4):
        ff_loads[k].start()
        i_loads[k].start()

    peers = [(y, 1 - c), (3 - y, 0), (3 - y, 1)]

    def sf_src(y_, c_, s):
        return sf.at[:, ds((2 * s + c_) * 4 + (y_ // 2) * 2 + y_ % 2, CB)]

    def sf_row(s, r, q):
        return sf_r.at[s, pl.ds(pl.multiple_of(r * RK + q * QR, QR), QR), :]

    for n, s in enumerate((s0, s1)):
        dst, rs = sf_r.at[s, ds(r4, RK), :], sf_rs.at[r4 * 2 + s]
        pltpu.make_async_copy(sf_src(y, c, s), dst, rs).start()
        send(remote(sf_src(y, 1 - c, s), dst, sf_ss.at[n], rs, dev(x, y, z, 1 - c)))
    for m, (y_, c_) in enumerate(peers[1:]):
        src = sf_src(y_, c_, s0).at[ds(z, QR), :]
        send(remote(src, sf_row(s0, r4, z), sf_ss.at[2 + m], sq_rs.at[r4 * 4 + z], dev(x, y_, z, c_)))

    def sf_far():
        for m, (y_, c_) in enumerate(peers[1:]):
            dst, rs = sf_r.at[s1, ds(r4, RK), :], sf_rs.at[r4 * 2 + s1]
            send(remote(sf_src(y_, c_, s1), dst, sf_ss.at[4 + m], rs, dev(x, y_, z, c_)))

    def sf_onward():
        for m in range(2):
            r = (1 - yh) * 2 + m
            unit, rs = sf_row(s0, r, z), sq_rs.at[r * 4 + z]
            arrived(unit, rs)
            for k in (2, 1, 3):
                send(remote(unit, unit, sf_ss.at[6 + m * 3 + k - 1], rs, z_dev((z + k) % 4)))

    def sf_wait_s0():
        for m in range(2):
            r = yh * 2 + m
            arrived(sf_r.at[s0, ds(r, RK), :], sf_rs.at[r * 2 + s0])
            r = (1 - yh) * 2 + m
            for k in range(1, 4):
                q = (z + k) % 4
                arrived(sf_row(s0, r, q), sq_rs.at[r * 4 + q])

    for k in range(4):
        dst = ffx.at[k, :, ds(r4, RK)]
        pltpu.make_async_copy(ff.at[k, r4], dst, fx_rs.at[k * 4 + r4]).start()
        send(remote(ff.at[k, yh * 2 + 1 - c], dst, fx_ss.at[k], fx_rs.at[k * 4 + r4], dev(x, y, z, 1 - c)))
    x_far = (x + 2 + z % 2) % 4

    def fx_half(to, h, r):
        return ffx.at[to, ds(h, FB // 2), ds(r, RK)]

    for m, (y_, c_) in enumerate(peers[1:]):
        src = ff.at[x_far, (y_ // 2) * 2 + c_, ds(z // 2, FB // 2)]
        send(remote(src, fx_half(x_far, z // 2, r4), fx_ss.at[4 + m], fxh_rs.at[z * 4 + r4], dev(x, y_, z, c_)))

    def fx_onward():
        for m in range(2):
            r = (1 - yh) * 2 + m
            unit, rs = fx_half(x_far, z // 2, r), fxh_rs.at[z * 4 + r]
            arrived(unit, rs)
            for k in (2, 1, 3):
                send(remote(unit, unit, fx_ss.at[6 + m * 3 + k - 1], rs, z_dev((z + k) % 4)))

    def fx_near(k):
        to = (x + k) % 4
        for m, (y_, c_) in enumerate(peers[1:]):
            dst, rs = ffx.at[to, :, ds(r4, RK)], fx_rs.at[to * 4 + r4]
            send(remote(ff.at[to, (y_ // 2) * 2 + c_], dst, fx_ss.at[12 + k * 2 + m], rs, dev(x, y_, z, c_)))

    h_acc[...] = jnp.zeros_like(h_acc)
    for k in range(4):
        ff_loads[k].wait()
        i_loads[k].wait()

        def h_step(j, _, k=k):
            h_acc[...] += nn(i_v[:, ds(k * 4 + j, FB)], ff_v[k, j])
            return 0

        lax.fori_loop(0, 4, h_step, 0)
    ht_mine = ht.at[ds(r4, RK), ds(yl, TOK)]
    ht_mine[...] = h_acc[...].T.astype(BF)
    for j in range(1, 8):
        other = (line + j) % 8
        send(remote(ht_mine, ht_mine, h_ss.at[j], h_rs.at[line], dev(x, other // 2, z, other % 2)))

    sf_far()
    sf_onward()
    fx_near(1)

    rg_acc[...] = jnp.zeros_like(rg_acc)

    def sf_wait(s):
        for q in range(4):
            arrived(sf_r.at[s, q * RK : (q + 1) * RK, :], sf_rs.at[q * 2 + s])

    def block(s, t):
        arrived(og_r.at[s, ds(t, TOK), :], og_rs.at[s * 2 + t])

    def rg_block(s, t):
        def step(n, _):
            rg_acc[t, n] += nt(og_r[s, ds(t, TOK), :], sf_r[s, ds(n, 256), :])
            return 0

        lax.fori_loop(0, 2, step, 0)

    sgs = {}
    for name, s in (("s0", s0), ("s1", s1)):
        sgs[name] = RingSum(z, z_dev, lambda q, s=s: sg_p.at[s, q], RK, sg_m.at[s], sg_r.at[s], sg_ss, sg_rs, s * 6)

    def sg_block(name, s):
        def step(i, _):
            q = (z + steps(i)) % 4
            sg_p[s, q] = nn(ht[ds(q, RK), :], og_r[s]).astype(BF)
            sgs[name].part_done(i)
            return 0

        lax.fori_loop(0, 4, step, 0)

    def pick(u, v):
        return jnp.where(root, u, v)

    def onward(i, s, t):
        src = og_r.at[s, ds(t, TOK), :]
        from_left = (2 * s + c) == left
        mine = root & (s == s0) & (t != yl)
        ahead = jnp.logical_not(root) & (t == 0) & from_left
        back = jnp.logical_not(root) & (t == 1) & jnp.logical_not(from_left)
        rs = og_rs.at[s * 2 + t]
        send(remote(src, src, fwd_ss.at[i * 2], rs, dev(right, y, z, c)), mine | ahead)
        send(remote(src, src, fwd_ss.at[i * 2 + 1], rs, dev(left, y, z, c)), mine | back)

    order = [(s0, yl), (pick(s0, s1), pick(1 - yl, yl)), (pick(s1, s0), pick(yl, 1 - yl)), (s1, 1 - yl)]
    block(*order[0])
    onward(0, *order[0])
    block(*order[1])
    onward(1, *order[1])
    fx_onward()
    sf_wait_s0()
    rg_block(*order[0])
    for j in range(1, 8):
        other = (line + j) % 8
        y_, c_ = other // 2, other % 2
        arrived(ht.at[ds((y_ // 2) * 2 + c_, RK), ds(y_ % 2, TOK)], h_rs.at[other])

    @pl.when(root)
    def _():
        sg_block("s0", s0)

    block(*order[2])
    onward(2, *order[2])
    rg_block(s0, 1 - yl)

    @pl.when(jnp.logical_not(root))
    def _():
        sg_block("s0", s0)

    sgs["s0"].merge()
    block(*order[3])
    onward(3, *order[3])
    sf_wait(s1)
    rg_block(s1, yl)
    rg_block(s1, 1 - yl)

    for t in range(2):
        for n in range(2):
            rg_p[t, :, n * 256 : (n + 1) * 256] = rg_acc[t, n].astype(BF)
    for j in range(1, 8):
        other = (line + j) % 8
        y_, c_ = other // 2, other % 2
        send(
            remote(
                rg_p.at[y_ % 2, :, ds((y_ // 2) * 2 + c_, RK)], rg_r.at[line], rg_ss.at[j], rg_rs.at[line],
                dev(x, y_, z, c_),
            )
        )

    fx_near(0)
    sg_block("s1", s1)

    def c8_send(name, s):
        sgs[name].wait()
        sg_s[s] = (sg_p[s, z].astype(F32) + sg_r[s, 0].astype(F32) + sg_r[s, 1].astype(F32)).astype(BF)
        dst = sg_out.at[:, ds(yl, CB)]
        to = (x, 2 * (z // 2) + s, 2 * c + yh, z % 2)
        near = pltpu.make_async_copy(sg_s.at[s], dst, c8_rs.at[yl])
        send(remote(sg_s.at[s], dst, c8_ss.at[s], c8_rs.at[yl], dev(*to)), jnp.logical_not(is_me(to)))
        pl.when(is_me(to))(near.start)

    c8_send("s0", s0)

    total = rg_p[yl, :, ds(r4, RK)].astype(F32)
    for j in range(1, 8):
        other = (line + j) % 8
        arrived(rg_r.at[other], rg_rs.at[other])
        total = total + rg_r[other].astype(F32)
    rg_mine = rg_all.at[:, ds(r4, RK)]
    rg_mine[...] = total.astype(BF)
    for n, (y_, c_) in enumerate([(y, 1 - c), ((y + 2) % 4, 0), ((y + 2) % 4, 1)]):
        send(remote(rg_mine, rg_mine, ra_ss.at[n], ra_rs.at[r4], dev(x, y_, z, c_)))
    rgt[...] = total.T.astype(BF)

    def fg_unit(own, z_, half):
        u = (pick_yl(own) * 4 + z_) * 2 + half
        fg_p[u] = nn(rgt[...], i_v[:, ds(u, FB)]).astype(BF)
        return u

    def pick_yl(own):
        return yl if own else 1 - yl

    fgs = [
        RingSum(
            z, z_dev, lambda z_, n=n, o=o: fg_p.at[(pick_yl(o) * 4 + z_) * 2 + n // 2], RK,
            fg_m.at[n], fg_z.at[n], fz_ss, fz_rs, n * 6,
        )
        for n, o in ((0, True), (1, False), (2, True))
    ]

    def y_copy(u, z_):
        return remote(fg_p.at[u], fg_y.at[z_], fy_ss.at[z_], fy_rs.at[z_], dev(x, yp, z, c))

    def p2(i, _):
        z_ = (z + i + 2) % 4
        y_copy(fg_unit(False, z_, 1), z_).start()
        return 0

    lax.fori_loop(0, 4, p2, 0)
    sgs["s1"].merge()
    for own in (False, True):
        zs = fgs[0 if own else 1]

        def first(i, _, own=own, zs=zs):
            fg_unit(own, (z + steps(i)) % 4, 0)
            zs.part_done(i)
            return 0

        lax.fori_loop(0, 4, first, 0)

    def o2(z_, _):
        fg_unit(True, z_, 1)
        return 0

    lax.fori_loop(0, 4, o2, 0)

    for j in range(1, 4):
        other = (r4 + j) % 4
        arrived(rg_all.at[:, ds(other, RK)], ra_rs.at[other])

    igs = RingSum(x, lambda to: dev(to, y, z, c), lambda x_: ig_p.at[x_], TOK, ig_m, ig_r, ig_ss, ig_rs, 0)

    def ig_part(i, _):
        to = (x + steps(i)) % 4
        for j in range(4):

            @pl.when((i >= 2) | (j // 2 == yh))
            def _(j=j):
                arrived(ffx.at[to, :, j * RK : (j + 1) * RK], fx_rs.at[to * 4 + j])

            for h in range(2):

                @pl.when((i < 2) & (j // 2 != yh) & (i + 2 * h != z))
                def _(j=j, h=h):
                    arrived(fx_half(to, h, j), fxh_rs.at[(i + 2 * h) * 4 + j])

        ig_p[to] = nt(rg_all[...], ffx[to]).astype(BF)
        igs.part_done(i)
        return 0

    lax.fori_loop(0, 4, ig_part, 0)
    fgs[1].merge()
    fgs[0].merge()
    c8_send("s1", s1)

    igs.merge()

    def merge(i, _):
        z_ = (z + steps(i)) % 4
        u = (yl * 4 + z_) * 2 + 1
        arrived(fg_y.at[z_], fy_rs.at[z_])
        fg_p[u] = (fg_p[u].astype(F32) + fg_y[z_].astype(F32)).astype(BF)
        fgs[2].part_done(i)
        return 0

    lax.fori_loop(0, 4, merge, 0)

    fgs[1].wait()
    total = fg_p[((1 - yl) * 4 + z) * 2].astype(F32) + fg_z[1, 0].astype(F32) + fg_z[1, 1].astype(F32)
    fg_f[0] = total.astype(BF)
    send(remote(fg_f.at[0], fg_f.at[1], ff_ss.at[0], ff_rs.at[0], dev(x, yp, z, c)))
    fgs[2].merge()


    igs.wait()

    def ig_sum(k, _):
        rows = ds(k, 64)
        acc = ig_p[x, rows, :].astype(F32) + ig_r[0, rows, :].astype(F32) + ig_r[1, rows, :].astype(F32)
        ig_out[rows, :] = acc.astype(BF)
        return 0

    lax.fori_loop(0, TOK // 64, ig_sum, 0)

    for half in range(2):
        kind = 2 * half
        fgs[kind].wait()
        if half == 0:
            arrived(fg_f.at[1], ff_rs.at[0])

        def fg_sum(k, _, half=half, kind=kind):
            cols = ds(k, 256)
            acc = fg_p[d * 2 + half, :, cols].astype(F32)
            for j in range(2):
                acc = acc + fg_z[kind, j, :, cols].astype(F32)
            if half == 0:
                acc = acc + fg_f[1, :, cols].astype(F32)
            fg_out[ds(half * 4 + k, 256), :] = acc.T.astype(BF)
            return 0

        lax.fori_loop(0, FB // 256, fg_sum, 0)

    for s in range(2):
        arrived(sg_out.at[:, s * CB : (s + 1) * CB], c8_rs.at[s])

    for cond, cp in sends:
        if cond is None:
            cp.wait_send()
        else:
            pl.when(cond)(cp.wait_send)
    for zs in list(sgs.values()) + fgs + [igs]:
        zs.drain()
    for z_ in range(4):
        y_copy(((1 - yl) * 4 + z_) * 2 + 1, z_).wait_send()


def place(a, b, c, a_out, b_out, c_out):
    a_out[...] = a[...]
    b_out[...] = b[...]
    c_out[...] = c[...]


def shards(inputs, first_factor, second_factor, out_grad):
    ff = first_factor.reshape(4, 4, FB, RK)
    any_ = pl.BlockSpec(memory_space=pl.ANY)
    vmem = pl.BlockSpec(memory_space=pltpu.VMEM)
    dma = pltpu.SemaphoreType.DMA
    results = pl.pallas_call(
        kernel,
        name="backward",
        out_shape=(
            jax.ShapeDtypeStruct((TOK, FB), BF),
            jax.ShapeDtypeStruct((DB, RK), BF),
            jax.ShapeDtypeStruct((RK, 2 * CB), BF),
        ),
        in_specs=[any_] * 4,
        out_specs=(vmem, vmem, vmem),
        scratch_shapes=[
            pltpu.VMEM((TOK, D), BF),
            pltpu.VMEM((4, 4, FB, RK), BF),
            pltpu.VMEM((2, 2 * TOK, CB), BF),
            pltpu.VMEM((2, 4 * RK, CB), BF),
            pltpu.VMEM((4, FB, 4 * RK), BF),
            pltpu.VMEM((4 * RK, 2 * TOK), BF),
            pltpu.VMEM((TOK, RK), F32),
            pltpu.VMEM((2, 2, TOK, 256), F32),
            pltpu.VMEM((2, TOK, 4 * RK), BF),
            pltpu.VMEM((8, TOK, RK), BF),
            pltpu.VMEM((TOK, 4 * RK), BF),
            pltpu.VMEM((2, 4, RK, CB), BF),
            pltpu.VMEM((2, 2, RK // 2, CB), BF),
            pltpu.VMEM((2, 2, RK, CB), BF),
            pltpu.VMEM((2, RK, CB), BF),
            pltpu.VMEM((16, RK, FB), BF),
            pltpu.VMEM((4, RK, FB), BF),
            pltpu.VMEM((3, 2, RK // 2, FB), BF),
            pltpu.VMEM((3, 2, RK, FB), BF),
            pltpu.VMEM((2, RK, FB), BF),
            pltpu.VMEM((4, TOK, FB), BF),
            pltpu.VMEM((2, TOK // 2, FB), BF),
            pltpu.VMEM((2, TOK, FB), BF),
            pltpu.VMEM((RK, TOK), BF),
            dma((4,)), dma((4,)),
            dma((4,)), dma((4,)), dma((8,)),
            dma((12,)), dma((8,)), dma((16,)),
            dma((16,)), dma((16,)), dma((16,)),
            dma((8,)), dma((8,)),
            dma((8,)), dma((8,)),
            dma((3,)), dma((4,)),
            dma((12,)), dma((12,)),
            dma((2,)), dma((2,)),
            dma((4,)), dma((4,)),
            dma((18,)), dma((18,)),
            dma((1,)), dma((1,)),
            dma((6,)), dma((6,)),
        ],
        cost_estimate=pl.CostEstimate(flops=10_100_000_000, bytes_accessed=30_000_000, transcendentals=0),
        compiler_params=pltpu.CompilerParams(
            collective_id=0, has_side_effects=True, vmem_limit_bytes=63 * 1024 * 1024
        ),
    )(inputs, ff, second_factor, out_grad)
    return pl.pallas_call(
        place,
        name="place",
        out_shape=[jax.ShapeDtypeStruct(r.shape, r.dtype) for r in results],
        in_specs=[vmem] * 3,
        out_specs=[vmem] * 3,
    )(*results)


def solution(mesh):
    in_specs = (P("dp", None), P(None, "factor"), P("factor", None), P("dp", "factor"))
    out_specs = (P("dp", "factor"), P("dp", "factor"), P("factor", "dp"))
    return jax.shard_map(shards, mesh=mesh, in_specs=in_specs, out_specs=out_specs, check_vma=False)
```

```python
import functools

import jax
import jax.numpy as jnp
from jax import lax
from jax.experimental import pallas as pl
from jax.experimental.pallas import tpu as pltpu
from jax.sharding import PartitionSpec as P

MESH = pl.DeviceIdType.MESH
BF = jnp.bfloat16
F32 = jnp.float32
TOK = 384
D = 16384
RK = 128
QR = 32
CB = 1664
FB = 1024
DB = 2048


def ds(i, n):
    return pl.ds(pl.multiple_of(i * n, n), n)


def nn(a, b):
    return jnp.dot(a, b, preferred_element_type=F32)


def nt(a, b):
    return lax.dot_general(a, b, (((1,), (1,)), ((), ())), preferred_element_type=F32)


def kernel(
    inp, ff, sf, og,
    ig_out, fg_out, sg_out,
    i_v, ff_v, og_r, sf_r, ffx, ht, h_acc, rg_acc, rg_p, rg_r, rg_all,
    sg_p, sg_m, sg_r, sg_s, fg_p, fg_y, fg_m, fg_z, fg_f, ig_p, ig_m, ig_r, rgt,
    i_sem, ff_sem,
    og_ss, og_rs, fwd_ss, sf_ss, sf_rs, sq_rs, fx_ss, fx_rs, fxh_rs, h_ss, h_rs, rg_ss, rg_rs, ra_ss, ra_rs,
    sg_ss, sg_rs, c8_ss, c8_rs, fy_ss, fy_rs, fz_ss, fz_rs, ff_ss, ff_rs, ig_ss, ig_rs,
):
    d = lax.axis_index("dp")
    f = lax.axis_index("factor")
    yl, z = d // 4, d % 4
    x, yh, c = f // 4, (f // 2) % 2, f % 2
    y = 2 * yh + yl
    yp = 2 * yh + 1 - yl
    r4 = yh * 2 + c
    line = y * 2 + c
    root = c == x % 2
    s0, s1 = x // 2, 1 - x // 2

    def dev(x_, y_, z_, c_):
        return ((y_ % 2) * 4 + z_, x_ * 4 + (y_ // 2) * 2 + c_)

    def remote(src, dst, ss, rs, to):
        return pltpu.make_async_remote_copy(
            src_ref=src, dst_ref=dst, send_sem=ss, recv_sem=rs, device_id=to, device_id_type=MESH
        )

    def arrived(dst, rs):
        pltpu.make_async_copy(dst, dst, rs).wait()

    sends = []

    def send(cp, cond=None):
        if cond is None:
            cp.start()
        else:
            pl.when(cond)(cp.start)
        sends.append((cond, cp))

    class RingSum:
        def __init__(self, at, to_dev, part, rows, mid, out, ss, rs, base):
            far, up, down = (at + 2) % 4, (at + 1) % 4, (at + 3) % 4
            lo, hi = pl.ds(0, rows // 2), pl.ds(rows // 2, rows // 2)

            def cp(n, src, dst, to):
                return remote(src, dst, ss.at[base + n], rs.at[base + n], to_dev(to))

            self.mid = mid
            self.far = [cp(0, part(far).at[lo], mid.at[0], up), cp(1, part(far).at[hi], mid.at[1], down)]
            self.plain = [cp(2, part(up).at[hi], out.at[0, hi], up), cp(3, part(down).at[lo], out.at[1, lo], down)]
            self.merged = [cp(4, part(up).at[lo], out.at[0, lo], up), cp(5, part(down).at[hi], out.at[1, hi], down)]
            self.own = [part(up).at[lo], part(down).at[hi]]
            self.mids = [(mid.at[0], rs.at[base]), (mid.at[1], rs.at[base + 1])]
            self.outs = [
                (out.at[0, hi], rs.at[base + 2]), (out.at[1, lo], rs.at[base + 3]),
                (out.at[0, lo], rs.at[base + 4]), (out.at[1, hi], rs.at[base + 5]),
            ]

        def part_done(self, i):
            pl.when(i == 0)(self.send_far)
            pl.when(i == 1)(self.plain[1].start)
            pl.when(i == 2)(self.plain[0].start)

        def send_far(self):
            self.far[0].start()
            self.far[1].start()

        def merge(self):
            for n, own in enumerate(self.own):
                arrived(*self.mids[n])
                own[...] = (own[...].astype(F32) + self.mid[n].astype(F32)).astype(BF)
                self.merged[n].start()

        def wait(self):
            for ref, sem in self.outs:
                arrived(ref, sem)

        def drain(self):
            for cp in self.far + self.plain + self.merged:
                cp.wait_send()

    def steps(i):
        return jnp.where(i < 2, i + 2, 3 - i)

    def z_dev(to):
        return dev(x, y, to, c)

    c8_to = [(x, 2 * (z // 2) + s, 2 * c + yh, z % 2) for s in range(2)]
    c8_from = [(x, 2 * (z % 2) + s, 2 * yh + c, z // 2) for s in range(2)]

    def is_me(t):
        return (t[1] == y) & (t[2] == z) & (t[3] == c)

    barrier = pltpu.get_barrier_semaphore()

    def greet(*t):
        pl.semaphore_signal(barrier, inc=1, device_id=dev(*t), device_id_type=MESH)

    for j in range(1, 8):
        other = (line + j) % 8
        greet(x, other // 2, z, other % 2)
    for k in range(1, 4):
        for cc in range(2):
            greet((x + k) % 4, y, z, cc)
    for k in range(1, 4):
        greet(x, y, (z + k) % 4, c)
    extra = 0
    for t in c8_to + c8_from:
        away = jnp.logical_not(is_me(t))

        @pl.when(away)
        def _(t=t):
            greet(*t)

        extra = extra + away.astype(jnp.int32)
    pl.semaphore_wait(barrier, 16 + extra)

    stays = c == yl
    moves = jnp.logical_not(stays)
    right, left = (x + 1) % 4, (x + 3) % 4
    og_dst = og_r.at[s0, ds(yl, TOK), :]
    og_rsem = og_rs.at[s0 * 2 + yl]
    send(remote(og, og_dst, og_ss.at[0], og_rsem, dev(right, y, z, x % 2)), stays)
    send(remote(og, og_dst, og_ss.at[1], og_rsem, dev(left, y, z, x % 2)), stays)
    send(remote(og, og_dst, og_ss.at[2], og_rsem, dev(x, yp, z, x % 2)), moves)
    send(remote(og, og_dst, og_ss.at[3], og_rsem, dev(x, y, z, 1 - c)), stays & jnp.logical_not(root))

    @pl.when(stays & root)
    def _():
        pltpu.make_async_copy(og, og_dst, og_rsem).start()

    ff_loads = [pltpu.make_async_copy(ff.at[k], ff_v.at[k], ff_sem.at[k]) for k in range(4)]
    i_loads = [
        pltpu.make_async_copy(inp.at[:, k * 4096 : (k + 1) * 4096], i_v.at[:, k * 4096 : (k + 1) * 4096], i_sem.at[k])
        for k in range(4)
    ]
    for k in range(4):
        ff_loads[k].start()
        i_loads[k].start()

    peers = [(y, 1 - c), (3 - y, 0), (3 - y, 1)]

    def sf_src(y_, c_, s):
        return sf.at[:, ds((2 * s + c_) * 4 + (y_ // 2) * 2 + y_ % 2, CB)]

    def sf_row(s, r, q):
        return sf_r.at[s, pl.ds(pl.multiple_of(r * RK + q * QR, QR), QR), :]

    for n, s in enumerate((s0, s1)):
        dst, rs = sf_r.at[s, ds(r4, RK), :], sf_rs.at[r4 * 2 + s]
        pltpu.make_async_copy(sf_src(y, c, s), dst, rs).start()
        send(remote(sf_src(y, 1 - c, s), dst, sf_ss.at[n], rs, dev(x, y, z, 1 - c)))
    for m, (y_, c_) in enumerate(peers[1:]):
        src = sf_src(y_, c_, s0).at[ds(z, QR), :]
        send(remote(src, sf_row(s0, r4, z), sf_ss.at[2 + m], sq_rs.at[r4 * 4 + z], dev(x, y_, z, c_)))

    def sf_far():
        for m, (y_, c_) in enumerate(peers[1:]):
            dst, rs = sf_r.at[s1, ds(r4, RK), :], sf_rs.at[r4 * 2 + s1]
            send(remote(sf_src(y_, c_, s1), dst, sf_ss.at[4 + m], rs, dev(x, y_, z, c_)))

    def sf_onward():
        for m in range(2):
            r = (1 - yh) * 2 + m
            unit, rs = sf_row(s0, r, z), sq_rs.at[r * 4 + z]
            arrived(unit, rs)
            for k in (2, 1, 3):
                send(remote(unit, unit, sf_ss.at[6 + m * 3 + k - 1], rs, z_dev((z + k) % 4)))

    def sf_wait_s0():
        for m in range(2):
            r = yh * 2 + m
            arrived(sf_r.at[s0, ds(r, RK), :], sf_rs.at[r * 2 + s0])
            r = (1 - yh) * 2 + m
            for k in range(1, 4):
                q = (z + k) % 4
                arrived(sf_row(s0, r, q), sq_rs.at[r * 4 + q])

    for k in range(4):
        dst = ffx.at[k, :, ds(r4, RK)]
        pltpu.make_async_copy(ff.at[k, r4], dst, fx_rs.at[k * 4 + r4]).start()
        send(remote(ff.at[k, yh * 2 + 1 - c], dst, fx_ss.at[k], fx_rs.at[k * 4 + r4], dev(x, y, z, 1 - c)))
    x_far = (x + 2 + z % 2) % 4

    def fx_half(to, h, r):
        return ffx.at[to, ds(h, FB // 2), ds(r, RK)]

    for m, (y_, c_) in enumerate(peers[1:]):
        src = ff.at[x_far, (y_ // 2) * 2 + c_, ds(z // 2, FB // 2)]
        send(remote(src, fx_half(x_far, z // 2, r4), fx_ss.at[4 + m], fxh_rs.at[z * 4 + r4], dev(x, y_, z, c_)))

    def fx_onward():
        for m in range(2):
            r = (1 - yh) * 2 + m
            unit, rs = fx_half(x_far, z // 2, r), fxh_rs.at[z * 4 + r]
            arrived(unit, rs)
            for k in (2, 1, 3):
                send(remote(unit, unit, fx_ss.at[6 + m * 3 + k - 1], rs, z_dev((z + k) % 4)))

    def fx_near(k):
        to = (x + k) % 4
        for m, (y_, c_) in enumerate(peers[1:]):
            dst, rs = ffx.at[to, :, ds(r4, RK)], fx_rs.at[to * 4 + r4]
            send(remote(ff.at[to, (y_ // 2) * 2 + c_], dst, fx_ss.at[12 + k * 2 + m], rs, dev(x, y_, z, c_)))

    h_acc[...] = jnp.zeros_like(h_acc)
    for k in range(4):
        ff_loads[k].wait()
        i_loads[k].wait()

        def h_step(j, _, k=k):
            h_acc[...] += nn(i_v[:, ds(k * 4 + j, FB)], ff_v[k, j])
            return 0

        lax.fori_loop(0, 4, h_step, 0)
    ht_mine = ht.at[ds(r4, RK), ds(yl, TOK)]
    ht_mine[...] = h_acc[...].T.astype(BF)
    for j in range(1, 8):
        other = (line + j) % 8
        send(remote(ht_mine, ht_mine, h_ss.at[j], h_rs.at[line], dev(x, other // 2, z, other % 2)))

    sf_far()
    sf_onward()
    fx_near(1)

    rg_acc[...] = jnp.zeros_like(rg_acc)

    def sf_wait(s):
        for q in range(4):
            arrived(sf_r.at[s, q * RK : (q + 1) * RK, :], sf_rs.at[q * 2 + s])

    def block(s, t):
        arrived(og_r.at[s, ds(t, TOK), :], og_rs.at[s * 2 + t])

    def rg_block(s, t):
        def step(n, _):
            rg_acc[t, n] += nt(og_r[s, ds(t, TOK), :], sf_r[s, ds(n, 256), :])
            return 0

        lax.fori_loop(0, 2, step, 0)

    sgs = {}
    for name, s in (("s0", s0), ("s1", s1)):
        sgs[name] = RingSum(z, z_dev, lambda q, s=s: sg_p.at[s, q], RK, sg_m.at[s], sg_r.at[s], sg_ss, sg_rs, s * 6)

    def sg_block(name, s):
        def step(i, _):
            q = (z + steps(i)) % 4
            sg_p[s, q] = nn(ht[ds(q, RK), :], og_r[s]).astype(BF)
            sgs[name].part_done(i)
            return 0

        lax.fori_loop(0, 4, step, 0)

    def pick(u, v):
        return jnp.where(root, u, v)

    def onward_root():
        src, rs = og_r.at[s0, ds(1 - yl, TOK), :], og_rs.at[s0 * 2 + 1 - yl]
        send(remote(src, src, fwd_ss.at[0], rs, dev(right, y, z, c)), root)
        send(remote(src, src, fwd_ss.at[1], rs, dev(left, y, z, c)), root)

    leaf = jnp.logical_not(root)

    def onward_leaf(i, s, t):
        src, rs = og_r.at[s, ds(t, TOK), :], og_rs.at[s * 2 + t]
        from_left = (2 * s + c) == left
        ahead = leaf & (t == 0) & from_left
        back = leaf & (t == 1) & jnp.logical_not(from_left)
        send(remote(src, src, fwd_ss.at[2 + i * 2], rs, dev(right, y, z, c)), ahead)
        send(remote(src, src, fwd_ss.at[3 + i * 2], rs, dev(left, y, z, c)), back)

    block(s0, yl)
    block(pick(s0, s1), pick(1 - yl, yl))
    onward_root()
    fx_onward()
    sf_wait_s0()
    rg_block(s0, yl)
    for j in range(1, 8):
        other = (line + j) % 8
        y_, c_ = other // 2, other % 2
        arrived(ht.at[ds((y_ // 2) * 2 + c_, RK), ds(y_ % 2, TOK)], h_rs.at[other])

    @pl.when(root)
    def _():
        sg_block("s0", s0)
        rg_block(s0, 1 - yl)
        sgs["s0"].merge()

    @pl.when(leaf)
    def _():
        block(s0, 1 - yl)

    onward_leaf(0, s0, yl)
    onward_leaf(1, s1, yl)
    onward_leaf(2, s0, 1 - yl)

    @pl.when(leaf)
    def _():
        sg_block("s0", s0)
        block(s1, 1 - yl)

    onward_leaf(3, s1, 1 - yl)

    @pl.when(leaf)
    def _():
        sg_block("s1", s1)
        rg_block(s0, 1 - yl)
        sgs["s0"].merge()
        sgs["s1"].merge()

    @pl.when(root)
    def _():
        block(s1, yl)
        block(s1, 1 - yl)

    sf_wait(s1)
    rg_block(s1, yl)
    rg_block(s1, 1 - yl)

    for t in range(2):
        for n in range(2):
            rg_p[t, :, n * 256 : (n + 1) * 256] = rg_acc[t, n].astype(BF)
    for j in range(1, 8):
        other = (line + j) % 8
        y_, c_ = other // 2, other % 2
        send(
            remote(
                rg_p.at[y_ % 2, :, ds((y_ // 2) * 2 + c_, RK)], rg_r.at[line], rg_ss.at[j], rg_rs.at[line],
                dev(x, y_, z, c_),
            )
        )

    fx_near(0)

    @pl.when(root)
    def _():
        sg_block("s1", s1)


    def c8_send(name, s):
        sgs[name].wait()
        sg_s[s] = (sg_p[s, z].astype(F32) + sg_r[s, 0].astype(F32) + sg_r[s, 1].astype(F32)).astype(BF)
        dst = sg_out.at[:, ds(yl, CB)]
        to = (x, 2 * (z // 2) + s, 2 * c + yh, z % 2)
        near = pltpu.make_async_copy(sg_s.at[s], dst, c8_rs.at[yl])
        send(remote(sg_s.at[s], dst, c8_ss.at[s], c8_rs.at[yl], dev(*to)), jnp.logical_not(is_me(to)))
        pl.when(is_me(to))(near.start)

    c8_send("s0", s0)

    total = rg_p[yl, :, ds(r4, RK)].astype(F32)
    for j in range(1, 8):
        other = (line + j) % 8
        arrived(rg_r.at[other], rg_rs.at[other])
        total = total + rg_r[other].astype(F32)
    rg_mine = rg_all.at[:, ds(r4, RK)]
    rg_mine[...] = total.astype(BF)
    for n, (y_, c_) in enumerate([(y, 1 - c), ((y + 2) % 4, 0), ((y + 2) % 4, 1)]):
        send(remote(rg_mine, rg_mine, ra_ss.at[n], ra_rs.at[r4], dev(x, y_, z, c_)))
    rgt[...] = total.T.astype(BF)

    def fg_unit(own, z_, half):
        u = (pick_yl(own) * 4 + z_) * 2 + half
        fg_p[u] = nn(rgt[...], i_v[:, ds(u, FB)]).astype(BF)
        return u

    def pick_yl(own):
        return yl if own else 1 - yl

    fgs = [
        RingSum(
            z, z_dev, lambda z_, n=n, o=o: fg_p.at[(pick_yl(o) * 4 + z_) * 2 + n // 2], RK,
            fg_m.at[n], fg_z.at[n], fz_ss, fz_rs, n * 6,
        )
        for n, o in ((0, True), (1, False), (2, True))
    ]

    def y_copy(u, z_):
        return remote(fg_p.at[u], fg_y.at[z_], fy_ss.at[z_], fy_rs.at[z_], dev(x, yp, z, c))

    def p2(i, _):
        z_ = (z + i + 2) % 4
        y_copy(fg_unit(False, z_, 1), z_).start()
        return 0

    lax.fori_loop(0, 4, p2, 0)
    pl.when(root)(sgs["s1"].merge)
    for own in (False, True):
        zs = fgs[0 if own else 1]

        def first(i, _, own=own, zs=zs):
            fg_unit(own, (z + steps(i)) % 4, 0)
            zs.part_done(i)
            return 0

        lax.fori_loop(0, 4, first, 0)

    def o2(z_, _):
        fg_unit(True, z_, 1)
        return 0

    lax.fori_loop(0, 4, o2, 0)

    for j in range(1, 4):
        other = (r4 + j) % 4
        arrived(rg_all.at[:, ds(other, RK)], ra_rs.at[other])

    igs = RingSum(x, lambda to: dev(to, y, z, c), lambda x_: ig_p.at[x_], TOK, ig_m, ig_r, ig_ss, ig_rs, 0)

    def ig_part(i, _):
        to = (x + steps(i)) % 4
        for j in range(4):

            @pl.when((i >= 2) | (j // 2 == yh))
            def _(j=j):
                arrived(ffx.at[to, :, j * RK : (j + 1) * RK], fx_rs.at[to * 4 + j])

            for h in range(2):

                @pl.when((i < 2) & (j // 2 != yh) & (i + 2 * h != z))
                def _(j=j, h=h):
                    arrived(fx_half(to, h, j), fxh_rs.at[(i + 2 * h) * 4 + j])

        ig_p[to] = nt(rg_all[...], ffx[to]).astype(BF)
        igs.part_done(i)
        return 0

    lax.fori_loop(0, 4, ig_part, 0)
    fgs[1].merge()
    fgs[0].merge()
    c8_send("s1", s1)

    igs.merge()

    def merge(i, _):
        z_ = (z + steps(i)) % 4
        u = (yl * 4 + z_) * 2 + 1
        arrived(fg_y.at[z_], fy_rs.at[z_])
        fg_p[u] = (fg_p[u].astype(F32) + fg_y[z_].astype(F32)).astype(BF)
        fgs[2].part_done(i)
        return 0

    lax.fori_loop(0, 4, merge, 0)

    fgs[1].wait()
    total = fg_p[((1 - yl) * 4 + z) * 2].astype(F32) + fg_z[1, 0].astype(F32) + fg_z[1, 1].astype(F32)
    fg_f[0] = total.astype(BF)
    send(remote(fg_f.at[0], fg_f.at[1], ff_ss.at[0], ff_rs.at[0], dev(x, yp, z, c)))
    fgs[2].merge()


    igs.wait()

    def ig_sum(k, _):
        rows = ds(k, 64)
        acc = ig_p[x, rows, :].astype(F32) + ig_r[0, rows, :].astype(F32) + ig_r[1, rows, :].astype(F32)
        ig_out[rows, :] = acc.astype(BF)
        return 0

    lax.fori_loop(0, TOK // 64, ig_sum, 0)

    for half in range(2):
        kind = 2 * half
        fgs[kind].wait()
        if half == 0:
            arrived(fg_f.at[1], ff_rs.at[0])

        def fg_sum(k, _, half=half, kind=kind):
            cols = ds(k, 256)
            acc = fg_p[d * 2 + half, :, cols].astype(F32)
            for j in range(2):
                acc = acc + fg_z[kind, j, :, cols].astype(F32)
            if half == 0:
                acc = acc + fg_f[1, :, cols].astype(F32)
            fg_out[ds(half * 4 + k, 256), :] = acc.T.astype(BF)
            return 0

        lax.fori_loop(0, FB // 256, fg_sum, 0)

    for s in range(2):
        arrived(sg_out.at[:, s * CB : (s + 1) * CB], c8_rs.at[s])

    for cond, cp in sends:
        if cond is None:
            cp.wait_send()
        else:
            pl.when(cond)(cp.wait_send)
    for zs in list(sgs.values()) + fgs + [igs]:
        zs.drain()
    for z_ in range(4):
        y_copy(((1 - yl) * 4 + z_) * 2 + 1, z_).wait_send()


def place(a, b, c, a_out, b_out, c_out):
    a_out[...] = a[...]
    b_out[...] = b[...]
    c_out[...] = c[...]


def shards(inputs, first_factor, second_factor, out_grad):
    ff = first_factor.reshape(4, 4, FB, RK)
    any_ = pl.BlockSpec(memory_space=pl.ANY)
    vmem = pl.BlockSpec(memory_space=pltpu.VMEM)
    dma = pltpu.SemaphoreType.DMA
    results = pl.pallas_call(
        kernel,
        name="backward",
        out_shape=(
            jax.ShapeDtypeStruct((TOK, FB), BF),
            jax.ShapeDtypeStruct((DB, RK), BF),
            jax.ShapeDtypeStruct((RK, 2 * CB), BF),
        ),
        in_specs=[any_] * 4,
        out_specs=(vmem, vmem, vmem),
        scratch_shapes=[
            pltpu.VMEM((TOK, D), BF),
            pltpu.VMEM((4, 4, FB, RK), BF),
            pltpu.VMEM((2, 2 * TOK, CB), BF),
            pltpu.VMEM((2, 4 * RK, CB), BF),
            pltpu.VMEM((4, FB, 4 * RK), BF),
            pltpu.VMEM((4 * RK, 2 * TOK), BF),
            pltpu.VMEM((TOK, RK), F32),
            pltpu.VMEM((2, 2, TOK, 256), F32),
            pltpu.VMEM((2, TOK, 4 * RK), BF),
            pltpu.VMEM((8, TOK, RK), BF),
            pltpu.VMEM((TOK, 4 * RK), BF),
            pltpu.VMEM((2, 4, RK, CB), BF),
            pltpu.VMEM((2, 2, RK // 2, CB), BF),
            pltpu.VMEM((2, 2, RK, CB), BF),
            pltpu.VMEM((2, RK, CB), BF),
            pltpu.VMEM((16, RK, FB), BF),
            pltpu.VMEM((4, RK, FB), BF),
            pltpu.VMEM((3, 2, RK // 2, FB), BF),
            pltpu.VMEM((3, 2, RK, FB), BF),
            pltpu.VMEM((2, RK, FB), BF),
            pltpu.VMEM((4, TOK, FB), BF),
            pltpu.VMEM((2, TOK // 2, FB), BF),
            pltpu.VMEM((2, TOK, FB), BF),
            pltpu.VMEM((RK, TOK), BF),
            dma((4,)), dma((4,)),
            dma((4,)), dma((4,)), dma((10,)),
            dma((12,)), dma((8,)), dma((16,)),
            dma((16,)), dma((16,)), dma((16,)),
            dma((8,)), dma((8,)),
            dma((8,)), dma((8,)),
            dma((3,)), dma((4,)),
            dma((12,)), dma((12,)),
            dma((2,)), dma((2,)),
            dma((4,)), dma((4,)),
            dma((18,)), dma((18,)),
            dma((1,)), dma((1,)),
            dma((6,)), dma((6,)),
        ],
        cost_estimate=pl.CostEstimate(flops=10_100_000_000, bytes_accessed=30_000_000, transcendentals=0),
        compiler_params=pltpu.CompilerParams(
            collective_id=0, has_side_effects=True, vmem_limit_bytes=63 * 1024 * 1024
        ),
    )(inputs, ff, second_factor, out_grad)
    return pl.pallas_call(
        place,
        name="place",
        out_shape=[jax.ShapeDtypeStruct(r.shape, r.dtype) for r in results],
        in_specs=[vmem] * 3,
        out_specs=[vmem] * 3,
    )(*results)


def solution(mesh):
    in_specs = (P("dp", None), P(None, "factor"), P("factor", None), P("dp", "factor"))
    out_specs = (P("dp", "factor"), P("dp", "factor"), P("factor", "dp"))
    return jax.shard_map(shards, mesh=mesh, in_specs=in_specs, out_specs=out_specs, check_vma=False)
```

```python
import functools

import jax
import jax.numpy as jnp
from jax import lax
from jax.experimental import pallas as pl
from jax.experimental.pallas import tpu as pltpu
from jax.sharding import PartitionSpec as P

MESH = pl.DeviceIdType.MESH
BF = jnp.bfloat16
F32 = jnp.float32
TOK = 384
D = 16384
RK = 128
QR = 32
CB = 1664
FB = 1024
DB = 2048


def ds(i, n):
    return pl.ds(pl.multiple_of(i * n, n), n)


def nn(a, b):
    return jnp.dot(a, b, preferred_element_type=F32)


def nt(a, b):
    return lax.dot_general(a, b, (((1,), (1,)), ((), ())), preferred_element_type=F32)


def kernel(
    inp, ff, sf, og,
    ig_out, fg_out, sg_out,
    i_v, ff_v, og_r, sf_r, ffx, ht, h_acc, rg_acc, rg_p, rg_r, rg_all,
    sg_p, sg_m, sg_r, sg_s, fg_p, fg_y, fg_m, fg_z, fg_f, ig_p, ig_m, ig_r, rgt,
    i_sem, ff_sem,
    og_ss, og_rs, fwd_ss, sf_ss, sf_rs, sq_rs, fx_ss, fx_rs, fxh_rs, h_ss, h_rs, rg_ss, rg_rs, ra_ss, ra_rs,
    sg_ss, sg_rs, c8_ss, c8_rs, fy_ss, fy_rs, fz_ss, fz_rs, ff_ss, ff_rs, ig_ss, ig_rs,
):
    d = lax.axis_index("dp")
    f = lax.axis_index("factor")
    yl, z = d // 4, d % 4
    x, yh, c = f // 4, (f // 2) % 2, f % 2
    y = 2 * yh + yl
    yp = 2 * yh + 1 - yl
    r4 = yh * 2 + c
    line = y * 2 + c
    root = c == x % 2
    s0, s1 = x // 2, 1 - x // 2

    def dev(x_, y_, z_, c_):
        return ((y_ % 2) * 4 + z_, x_ * 4 + (y_ // 2) * 2 + c_)

    def remote(src, dst, ss, rs, to):
        return pltpu.make_async_remote_copy(
            src_ref=src, dst_ref=dst, send_sem=ss, recv_sem=rs, device_id=to, device_id_type=MESH
        )

    def arrived(dst, rs):
        pltpu.make_async_copy(dst, dst, rs).wait()

    sends = []

    def send(cp, cond=None):
        if cond is None:
            cp.start()
        else:
            pl.when(cond)(cp.start)
        sends.append((cond, cp))

    class RingSum:
        def __init__(self, at, to_dev, part, rows, mid, out, ss, rs, base):
            far, up, down = (at + 2) % 4, (at + 1) % 4, (at + 3) % 4
            lo, hi = pl.ds(0, rows // 2), pl.ds(rows // 2, rows // 2)

            def cp(n, src, dst, to):
                return remote(src, dst, ss.at[base + n], rs.at[base + n], to_dev(to))

            self.mid = mid
            self.far = [cp(0, part(far).at[lo], mid.at[0], up), cp(1, part(far).at[hi], mid.at[1], down)]
            self.plain = [cp(2, part(up).at[hi], out.at[0, hi], up), cp(3, part(down).at[lo], out.at[1, lo], down)]
            self.merged = [cp(4, part(up).at[lo], out.at[0, lo], up), cp(5, part(down).at[hi], out.at[1, hi], down)]
            self.own = [part(up).at[lo], part(down).at[hi]]
            self.mids = [(mid.at[0], rs.at[base]), (mid.at[1], rs.at[base + 1])]
            self.outs = [
                (out.at[0, hi], rs.at[base + 2]), (out.at[1, lo], rs.at[base + 3]),
                (out.at[0, lo], rs.at[base + 4]), (out.at[1, hi], rs.at[base + 5]),
            ]

        def part_done(self, i):
            pl.when(i == 0)(self.send_far)
            pl.when(i == 1)(self.plain[1].start)
            pl.when(i == 2)(self.plain[0].start)

        def send_far(self):
            self.far[0].start()
            self.far[1].start()

        def merge(self):
            for n, own in enumerate(self.own):
                arrived(*self.mids[n])
                own[...] = (own[...].astype(F32) + self.mid[n].astype(F32)).astype(BF)
                self.merged[n].start()

        def wait(self):
            for ref, sem in self.outs:
                arrived(ref, sem)

        def drain(self):
            for cp in self.far + self.plain + self.merged:
                cp.wait_send()

    def steps(i):
        return jnp.where(i < 2, i + 2, 3 - i)

    def z_dev(to):
        return dev(x, y, to, c)

    c8_to = [(x, 2 * (z // 2) + s, 2 * c + yh, z % 2) for s in range(2)]
    c8_from = [(x, 2 * (z % 2) + s, 2 * yh + c, z // 2) for s in range(2)]

    def is_me(t):
        return (t[1] == y) & (t[2] == z) & (t[3] == c)

    barrier = pltpu.get_barrier_semaphore()

    def greet(*t):
        pl.semaphore_signal(barrier, inc=1, device_id=dev(*t), device_id_type=MESH)

    for j in range(1, 8):
        other = (line + j) % 8
        greet(x, other // 2, z, other % 2)
    for k in range(1, 4):
        for cc in range(2):
            greet((x + k) % 4, y, z, cc)
    for k in range(1, 4):
        greet(x, y, (z + k) % 4, c)
    extra = 0
    for t in c8_to + c8_from:
        away = jnp.logical_not(is_me(t))

        @pl.when(away)
        def _(t=t):
            greet(*t)

        extra = extra + away.astype(jnp.int32)
    pl.semaphore_wait(barrier, 16 + extra)

    stays = c == yl
    moves = jnp.logical_not(stays)
    right, left = (x + 1) % 4, (x + 3) % 4
    og_dst = og_r.at[s0, ds(yl, TOK), :]
    og_rsem = og_rs.at[s0 * 2 + yl]
    send(remote(og, og_dst, og_ss.at[0], og_rsem, dev(right, y, z, x % 2)), stays)
    send(remote(og, og_dst, og_ss.at[1], og_rsem, dev(left, y, z, x % 2)), stays)
    send(remote(og, og_dst, og_ss.at[2], og_rsem, dev(x, yp, z, x % 2)), moves)
    send(remote(og, og_dst, og_ss.at[3], og_rsem, dev(x, y, z, 1 - c)), stays & jnp.logical_not(root))

    @pl.when(stays & root)
    def _():
        pltpu.make_async_copy(og, og_dst, og_rsem).start()

    ff_loads = [pltpu.make_async_copy(ff.at[k], ff_v.at[k], ff_sem.at[k]) for k in range(4)]
    i_loads = [
        pltpu.make_async_copy(inp.at[:, k * 4096 : (k + 1) * 4096], i_v.at[:, k * 4096 : (k + 1) * 4096], i_sem.at[k])
        for k in range(4)
    ]
    for k in range(4):
        ff_loads[k].start()
        i_loads[k].start()

    peers = [(y, 1 - c), (3 - y, 0), (3 - y, 1)]

    def sf_src(y_, c_, s):
        return sf.at[:, ds((2 * s + c_) * 4 + (y_ // 2) * 2 + y_ % 2, CB)]

    def sf_row(s, r, q):
        return sf_r.at[s, pl.ds(pl.multiple_of(r * RK + q * QR, QR), QR), :]

    for n, s in enumerate((s0, s1)):
        dst, rs = sf_r.at[s, ds(r4, RK), :], sf_rs.at[r4 * 2 + s]
        pltpu.make_async_copy(sf_src(y, c, s), dst, rs).start()
        send(remote(sf_src(y, 1 - c, s), dst, sf_ss.at[n], rs, dev(x, y, z, 1 - c)))
    for m, (y_, c_) in enumerate(peers[1:]):
        src = sf_src(y_, c_, s0).at[ds(z, QR), :]
        send(remote(src, sf_row(s0, r4, z), sf_ss.at[2 + m], sq_rs.at[r4 * 4 + z], dev(x, y_, z, c_)))

    def sf_far():
        for m, (y_, c_) in enumerate(peers[1:]):
            dst, rs = sf_r.at[s1, ds(r4, RK), :], sf_rs.at[r4 * 2 + s1]
            send(remote(sf_src(y_, c_, s1), dst, sf_ss.at[4 + m], rs, dev(x, y_, z, c_)))

    def sf_onward():
        for m in range(2):
            r = (1 - yh) * 2 + m
            unit, rs = sf_row(s0, r, z), sq_rs.at[r * 4 + z]
            arrived(unit, rs)
            for k in (2, 1, 3):
                send(remote(unit, unit, sf_ss.at[6 + m * 3 + k - 1], rs, z_dev((z + k) % 4)))

    def sf_wait_s0():
        for m in range(2):
            r = yh * 2 + m
            arrived(sf_r.at[s0, ds(r, RK), :], sf_rs.at[r * 2 + s0])
            r = (1 - yh) * 2 + m
            for k in range(1, 4):
                q = (z + k) % 4
                arrived(sf_row(s0, r, q), sq_rs.at[r * 4 + q])

    for k in range(4):
        dst = ffx.at[k, :, ds(r4, RK)]
        pltpu.make_async_copy(ff.at[k, r4], dst, fx_rs.at[k * 4 + r4]).start()
        send(remote(ff.at[k, yh * 2 + 1 - c], dst, fx_ss.at[k], fx_rs.at[k * 4 + r4], dev(x, y, z, 1 - c)))
    x_far = (x + 2 + z % 2) % 4

    def fx_half(to, h, r):
        return ffx.at[to, ds(h, FB // 2), ds(r, RK)]

    for m, (y_, c_) in enumerate(peers[1:]):
        src = ff.at[x_far, (y_ // 2) * 2 + c_, ds(z // 2, FB // 2)]
        send(remote(src, fx_half(x_far, z // 2, r4), fx_ss.at[4 + m], fxh_rs.at[z * 4 + r4], dev(x, y_, z, c_)))

    def fx_onward():
        for m in range(2):
            r = (1 - yh) * 2 + m
            unit, rs = fx_half(x_far, z // 2, r), fxh_rs.at[z * 4 + r]
            arrived(unit, rs)
            for k in (2, 1, 3):
                send(remote(unit, unit, fx_ss.at[6 + m * 3 + k - 1], rs, z_dev((z + k) % 4)))

    def fx_near(k):
        to = (x + k) % 4
        for m, (y_, c_) in enumerate(peers[1:]):
            dst, rs = ffx.at[to, :, ds(r4, RK)], fx_rs.at[to * 4 + r4]
            send(remote(ff.at[to, (y_ // 2) * 2 + c_], dst, fx_ss.at[12 + k * 2 + m], rs, dev(x, y_, z, c_)))

    h_acc[...] = jnp.zeros_like(h_acc)
    for k in range(4):
        ff_loads[k].wait()
        i_loads[k].wait()

        def h_step(j, _, k=k):
            h_acc[...] += nn(i_v[:, ds(k * 4 + j, FB)], ff_v[k, j])
            return 0

        lax.fori_loop(0, 4, h_step, 0)
    ht_mine = ht.at[ds(r4, RK), ds(yl, TOK)]
    ht_mine[...] = h_acc[...].T.astype(BF)
    for j in range(1, 8):
        other = (line + j) % 8
        send(remote(ht_mine, ht_mine, h_ss.at[j], h_rs.at[line], dev(x, other // 2, z, other % 2)))

    sf_far()
    sf_onward()
    fx_near(1)

    rg_acc[...] = jnp.zeros_like(rg_acc)

    def sf_wait(s):
        for q in range(4):
            arrived(sf_r.at[s, q * RK : (q + 1) * RK, :], sf_rs.at[q * 2 + s])

    def block(s, t):
        arrived(og_r.at[s, ds(t, TOK), :], og_rs.at[s * 2 + t])

    def rg_block(s, t):
        def step(n, _):
            rg_acc[t, n] += nt(og_r[s, ds(t, TOK), :], sf_r[s, ds(n, 256), :])
            return 0

        lax.fori_loop(0, 2, step, 0)

    sgs = {}
    for name, s in (("s0", s0), ("s1", s1)):
        sgs[name] = RingSum(z, z_dev, lambda q, s=s: sg_p.at[s, q], RK, sg_m.at[s], sg_r.at[s], sg_ss, sg_rs, s * 6)

    def sg_block(name, s):
        def step(i, _):
            q = (z + steps(i)) % 4
            sg_p[s, q] = nn(ht[ds(q, RK), :], og_r[s]).astype(BF)
            sgs[name].part_done(i)
            return 0

        lax.fori_loop(0, 4, step, 0)

    def pick(u, v):
        return jnp.where(root, u, v)

    def onward_root():
        src, rs = og_r.at[s0, ds(1 - yl, TOK), :], og_rs.at[s0 * 2 + 1 - yl]
        send(remote(src, src, fwd_ss.at[0], rs, dev(right, y, z, c)), root)
        send(remote(src, src, fwd_ss.at[1], rs, dev(left, y, z, c)), root)

    leaf = jnp.logical_not(root)

    def onward_leaf(i, s, t):
        src, rs = og_r.at[s, ds(t, TOK), :], og_rs.at[s * 2 + t]
        from_left = (2 * s + c) == left
        ahead = leaf & (t == 0) & from_left
        back = leaf & (t == 1) & jnp.logical_not(from_left)
        send(remote(src, src, fwd_ss.at[2 + i * 2], rs, dev(right, y, z, c)), ahead)
        send(remote(src, src, fwd_ss.at[3 + i * 2], rs, dev(left, y, z, c)), back)

    block(s0, yl)
    block(pick(s0, s1), pick(1 - yl, yl))
    onward_root()
    fx_onward()
    sf_wait_s0()
    rg_block(s0, yl)
    for j in range(1, 8):
        other = (line + j) % 8
        y_, c_ = other // 2, other % 2
        arrived(ht.at[ds((y_ // 2) * 2 + c_, RK), ds(y_ % 2, TOK)], h_rs.at[other])

    @pl.when(root)
    def _():
        sg_block("s0", s0)
        rg_block(s0, 1 - yl)
        sgs["s0"].merge()

    @pl.when(leaf)
    def _():
        block(s0, 1 - yl)

    onward_leaf(0, s0, yl)
    onward_leaf(1, s1, yl)
    onward_leaf(2, s0, 1 - yl)

    @pl.when(leaf)
    def _():
        sg_block("s0", s0)
        block(s1, 1 - yl)

    onward_leaf(3, s1, 1 - yl)

    @pl.when(leaf)
    def _():
        sg_block("s1", s1)
        rg_block(s0, 1 - yl)
        sgs["s0"].merge()
        sgs["s1"].merge()

    @pl.when(root)
    def _():
        block(s1, yl)
        block(s1, 1 - yl)

    sf_wait(s1)
    def rg_send(t, first):
        for n in range(2):
            rg_p[t, :, n * 256 : (n + 1) * 256] = rg_acc[t, n].astype(BF)
        for yy in range(2):
            for cc in range(2):
                if first or yy or cc:
                    y_ = 2 * ((yh + yy) % 2) + t
                    c_ = (c + cc) % 2
                    send(
                        remote(
                            rg_p.at[t, :, ds((y_ // 2) * 2 + c_, RK)], rg_r.at[line],
                            rg_ss.at[first * 4 + yy * 2 + cc], rg_rs.at[line], dev(x, y_, z, c_),
                        )
                    )

    rg_block(s1, 1 - yl)
    rg_send(1 - yl, 1)
    rg_block(s1, yl)
    rg_send(yl, 0)
    fx_near(0)

    @pl.when(root)
    def _():
        sg_block("s1", s1)


    def c8_send(name, s):
        sgs[name].wait()
        sg_s[s] = (sg_p[s, z].astype(F32) + sg_r[s, 0].astype(F32) + sg_r[s, 1].astype(F32)).astype(BF)
        dst = sg_out.at[:, ds(yl, CB)]
        to = (x, 2 * (z // 2) + s, 2 * c + yh, z % 2)
        near = pltpu.make_async_copy(sg_s.at[s], dst, c8_rs.at[yl])
        send(remote(sg_s.at[s], dst, c8_ss.at[s], c8_rs.at[yl], dev(*to)), jnp.logical_not(is_me(to)))
        pl.when(is_me(to))(near.start)


    total = rg_p[yl, :, ds(r4, RK)].astype(F32)
    for j in range(1, 8):
        other = (line + j) % 8
        arrived(rg_r.at[other], rg_rs.at[other])
        total = total + rg_r[other].astype(F32)
    rg_mine = rg_all.at[:, ds(r4, RK)]
    rg_mine[...] = total.astype(BF)
    for n, (y_, c_) in enumerate([(y, 1 - c), ((y + 2) % 4, 0), ((y + 2) % 4, 1)]):
        send(remote(rg_mine, rg_mine, ra_ss.at[n], ra_rs.at[r4], dev(x, y_, z, c_)))
    rgt[...] = total.T.astype(BF)

    def fg_unit(own, z_, half):
        u = (pick_yl(own) * 4 + z_) * 2 + half
        fg_p[u] = nn(rgt[...], i_v[:, ds(u, FB)]).astype(BF)
        return u

    def pick_yl(own):
        return yl if own else 1 - yl

    fgs = [
        RingSum(
            z, z_dev, lambda z_, n=n, o=o: fg_p.at[(pick_yl(o) * 4 + z_) * 2 + n // 2], RK,
            fg_m.at[n], fg_z.at[n], fz_ss, fz_rs, n * 6,
        )
        for n, o in ((0, True), (1, False), (2, True))
    ]

    def y_copy(u, z_):
        return remote(fg_p.at[u], fg_y.at[z_], fy_ss.at[z_], fy_rs.at[z_], dev(x, yp, z, c))

    def p2(i, _):
        z_ = (z + i + 2) % 4
        y_copy(fg_unit(False, z_, 1), z_).start()
        return 0

    lax.fori_loop(0, 4, p2, 0)
    pl.when(root)(sgs["s1"].merge)
    for own in (False, True):
        zs = fgs[0 if own else 1]

        def first(i, _, own=own, zs=zs):
            fg_unit(own, (z + steps(i)) % 4, 0)
            zs.part_done(i)
            return 0

        lax.fori_loop(0, 4, first, 0)

    def o2(z_, _):
        fg_unit(True, z_, 1)
        return 0

    lax.fori_loop(0, 4, o2, 0)
    c8_send("s0", s0)

    for j in range(1, 4):
        other = (r4 + j) % 4
        arrived(rg_all.at[:, ds(other, RK)], ra_rs.at[other])

    igs = RingSum(x, lambda to: dev(to, y, z, c), lambda x_: ig_p.at[x_], TOK, ig_m, ig_r, ig_ss, ig_rs, 0)

    def ig_part(i, _):
        to = (x + steps(i)) % 4
        for j in range(4):

            @pl.when((i >= 2) | (j // 2 == yh))
            def _(j=j):
                arrived(ffx.at[to, :, j * RK : (j + 1) * RK], fx_rs.at[to * 4 + j])

            for h in range(2):

                @pl.when((i < 2) & (j // 2 != yh) & (i + 2 * h != z))
                def _(j=j, h=h):
                    arrived(fx_half(to, h, j), fxh_rs.at[(i + 2 * h) * 4 + j])

        ig_p[to] = nt(rg_all[...], ffx[to]).astype(BF)
        igs.part_done(i)
        return 0

    lax.fori_loop(0, 4, ig_part, 0)
    fgs[1].merge()
    fgs[0].merge()
    c8_send("s1", s1)

    igs.merge()

    def merge(i, _):
        z_ = (z + steps(i)) % 4
        u = (yl * 4 + z_) * 2 + 1
        arrived(fg_y.at[z_], fy_rs.at[z_])
        fg_p[u] = (fg_p[u].astype(F32) + fg_y[z_].astype(F32)).astype(BF)
        fgs[2].part_done(i)
        return 0

    lax.fori_loop(0, 4, merge, 0)

    fgs[1].wait()
    total = fg_p[((1 - yl) * 4 + z) * 2].astype(F32) + fg_z[1, 0].astype(F32) + fg_z[1, 1].astype(F32)
    fg_f[0] = total.astype(BF)
    send(remote(fg_f.at[0], fg_f.at[1], ff_ss.at[0], ff_rs.at[0], dev(x, yp, z, c)))
    fgs[2].merge()


    igs.wait()

    def ig_sum(k, _):
        rows = ds(k, 64)
        acc = ig_p[x, rows, :].astype(F32) + ig_r[0, rows, :].astype(F32) + ig_r[1, rows, :].astype(F32)
        ig_out[rows, :] = acc.astype(BF)
        return 0

    lax.fori_loop(0, TOK // 64, ig_sum, 0)

    for half in range(2):
        kind = 2 * half
        fgs[kind].wait()
        if half == 0:
            arrived(fg_f.at[1], ff_rs.at[0])

        def fg_sum(k, _, half=half, kind=kind):
            cols = ds(k, 256)
            acc = fg_p[d * 2 + half, :, cols].astype(F32)
            for j in range(2):
                acc = acc + fg_z[kind, j, :, cols].astype(F32)
            if half == 0:
                acc = acc + fg_f[1, :, cols].astype(F32)
            fg_out[ds(half * 4 + k, 256), :] = acc.T.astype(BF)
            return 0

        lax.fori_loop(0, FB // 256, fg_sum, 0)

    for s in range(2):
        arrived(sg_out.at[:, s * CB : (s + 1) * CB], c8_rs.at[s])

    for cond, cp in sends:
        if cond is None:
            cp.wait_send()
        else:
            pl.when(cond)(cp.wait_send)
    for zs in list(sgs.values()) + fgs + [igs]:
        zs.drain()
    for z_ in range(4):
        y_copy(((1 - yl) * 4 + z_) * 2 + 1, z_).wait_send()


def place(a, b, c, a_out, b_out, c_out):
    a_out[...] = a[...]
    b_out[...] = b[...]
    c_out[...] = c[...]


def shards(inputs, first_factor, second_factor, out_grad):
    ff = first_factor.reshape(4, 4, FB, RK)
    any_ = pl.BlockSpec(memory_space=pl.ANY)
    vmem = pl.BlockSpec(memory_space=pltpu.VMEM)
    dma = pltpu.SemaphoreType.DMA
    results = pl.pallas_call(
        kernel,
        name="backward",
        out_shape=(
            jax.ShapeDtypeStruct((TOK, FB), BF),
            jax.ShapeDtypeStruct((DB, RK), BF),
            jax.ShapeDtypeStruct((RK, 2 * CB), BF),
        ),
        in_specs=[any_] * 4,
        out_specs=(vmem, vmem, vmem),
        scratch_shapes=[
            pltpu.VMEM((TOK, D), BF),
            pltpu.VMEM((4, 4, FB, RK), BF),
            pltpu.VMEM((2, 2 * TOK, CB), BF),
            pltpu.VMEM((2, 4 * RK, CB), BF),
            pltpu.VMEM((4, FB, 4 * RK), BF),
            pltpu.VMEM((4 * RK, 2 * TOK), BF),
            pltpu.VMEM((TOK, RK), F32),
            pltpu.VMEM((2, 2, TOK, 256), F32),
            pltpu.VMEM((2, TOK, 4 * RK), BF),
            pltpu.VMEM((8, TOK, RK), BF),
            pltpu.VMEM((TOK, 4 * RK), BF),
            pltpu.VMEM((2, 4, RK, CB), BF),
            pltpu.VMEM((2, 2, RK // 2, CB), BF),
            pltpu.VMEM((2, 2, RK, CB), BF),
            pltpu.VMEM((2, RK, CB), BF),
            pltpu.VMEM((16, RK, FB), BF),
            pltpu.VMEM((4, RK, FB), BF),
            pltpu.VMEM((3, 2, RK // 2, FB), BF),
            pltpu.VMEM((3, 2, RK, FB), BF),
            pltpu.VMEM((2, RK, FB), BF),
            pltpu.VMEM((4, TOK, FB), BF),
            pltpu.VMEM((2, TOK // 2, FB), BF),
            pltpu.VMEM((2, TOK, FB), BF),
            pltpu.VMEM((RK, TOK), BF),
            dma((4,)), dma((4,)),
            dma((4,)), dma((4,)), dma((10,)),
            dma((12,)), dma((8,)), dma((16,)),
            dma((16,)), dma((16,)), dma((16,)),
            dma((8,)), dma((8,)),
            dma((8,)), dma((8,)),
            dma((3,)), dma((4,)),
            dma((12,)), dma((12,)),
            dma((2,)), dma((2,)),
            dma((4,)), dma((4,)),
            dma((18,)), dma((18,)),
            dma((1,)), dma((1,)),
            dma((6,)), dma((6,)),
        ],
        cost_estimate=pl.CostEstimate(flops=10_100_000_000, bytes_accessed=30_000_000, transcendentals=0),
        compiler_params=pltpu.CompilerParams(
            collective_id=0, has_side_effects=True, vmem_limit_bytes=63 * 1024 * 1024
        ),
    )(inputs, ff, second_factor, out_grad)
    return pl.pallas_call(
        place,
        name="place",
        out_shape=[jax.ShapeDtypeStruct(r.shape, r.dtype) for r in results],
        in_specs=[vmem] * 3,
        out_specs=[vmem] * 3,
    )(*results)


def solution(mesh):
    in_specs = (P("dp", None), P(None, "factor"), P("factor", None), P("dp", "factor"))
    out_specs = (P("dp", "factor"), P("dp", "factor"), P("factor", "dp"))
    return jax.shard_map(shards, mesh=mesh, in_specs=in_specs, out_specs=out_specs, check_vma=False)
```
